128 devices in a mesh: grp: 4 (over z), sp: 32 (over y, x, core).
Axes of the slice: x: 4, y: 4, z: 4, core: 2. Of those that a mesh axis runs over, the one named last changes fastest.
Arguments:
- grad_out: bfloat16 [16384, 4096], P(('grp', 'sp')), may hold values from -3 to 3
- routes: int32 [16384, 8], P(('grp', 'sp')), may hold values from 0 to 63, as said below
- probs: bfloat16 [16384, 8], P(('grp', 'sp')), may hold values from 0.019897461 to 0.5
- hidden_act: bfloat16 [16384, 8, 768], P(('grp', 'sp')), may hold values from -1.5 to 1.5
- placement: int32 [4, 32], replicated, may hold values from 0 to 63, as said below
- down_weight: bfloat16 [64, 768, 4096], P('sp'), may hold values from -0.21875 to 0.21875
Outputs:
- grad_act: bfloat16 [16384, 8, 768], P(('grp', 'sp'))
- grad_prob: float32 [16384, 8], P(('grp', 'sp'))
- weight_grad: bfloat16 [4, 32, 768, 4096], P('grp', 'sp')
The draws below stay inside these ranges and needn't reach their ends.
Inputs may be any that keep to these rules, and one draw needn't show every extreme that they name: `routes`: each row names 8 different experts; among the 128 rows of one device no expert is named by more than 17 rows, and some expert by exactly 17 in some device's rows. placement[g, s] is 2 s or 2 s + 1, and each of these two experts stands in at least one of the 4 entries of column s.
All inputs are finite; a program needn't handle non-finite values.
Results may differ from the reference program's by a relative error of at most 0.007.
Values may be sent and summed in bfloat16 or wider, within the bound.
No kernel may reach another device: no remote copies, remote signals or barrier semaphores. Data moves between devices by JAX's collectives and lax.ppermute only.
A program may use at most 192 MiB of HBM per device.

```python
import math
import jax
import jax.numpy as jnp
from jax import lax

D = 4096
FFW = 768
TOP = 8
TOK_DEV = 128
EXPERTS = 64
MOST = 17
TOKENS = 16384
N_GRP = 4
N_SP = 32


def expert_rank(key):
    key = jax.random.fold_in(key, 11)
    by_rank = jax.random.permutation(key, EXPERTS)
    return jnp.argsort(by_rank).astype(jnp.int32)


def draw_routes(key, part):
    rank = expert_rank(key)
    key = jax.random.fold_in(key, 5)
    total = TOK_DEV * TOP
    base = total // EXPERTS
    step_size = MOST - base
    quarter = EXPERTS // 4
    top_half = rank < EXPERTS // 2
    blocks = N_GRP * N_SP

    def one_block(block_key):
        key_hot, key_cold, key_rows = jax.random.split(block_key, 3)
        score_hot = jax.random.randint(key_hot, (EXPERTS,), 0, 1 << 20) * EXPERTS + rank
        score_hot = jnp.where(top_half, score_hot, score_hot + (1 << 30))
        hot = jnp.argsort(jnp.argsort(score_hot)) < quarter
        score_cold = jax.random.randint(key_cold, (EXPERTS,), 0, 1 << 20) * EXPERTS + rank
        score_cold = jnp.where(top_half, score_cold + (1 << 30), score_cold)
        cold = jnp.argsort(jnp.argsort(score_cold)) < quarter
        counts = base + step_size * hot.astype(jnp.int32) - step_size * cold.astype(jnp.int32)
        ends = jnp.cumsum(counts)
        slots = jnp.arange(total)
        slot_expert = jnp.sum((slots[:, None] >= ends[None, :]).astype(jnp.int32), axis=1)
        table = slot_expert.reshape(TOP, TOK_DEV).T
        row_order = jax.random.permutation(key_rows, TOK_DEV)
        return table[row_order]
    keys = jax.random.split(key, blocks)
    result = jax.vmap(one_block)(keys)
    return result.reshape(blocks * TOK_DEV, TOP).astype(jnp.int32)


def draw_placement(key, part):
    rank = expert_rank(key)
    key = jax.random.fold_in(key, 7)
    key_count, key_order = jax.random.split(key)
    hot_count = jax.random.randint(key_count, (N_SP,), N_GRP // 2, N_GRP)
    low_hot = rank[0::2] < rank[1::2]
    low_count = jnp.where(low_hot, hot_count, N_GRP - hot_count)
    scores = jax.random.randint(key_order, (N_GRP, N_SP), 0, 1 << 20) * N_GRP + jnp.arange(N_GRP)[:, None]
    order_rank = jnp.argsort(jnp.argsort(scores, axis=0), axis=0)
    table = 2 * jnp.arange(N_SP)[None, :] + (order_rank >= low_count[None, :]).astype(jnp.int32)
    return table.astype(jnp.int32)


def levels(own_key, dims, cuts, smallest, high):
    loudness, own = 1.0, jax.random.fold_in(own_key, 6)
    for dim, blocks in cuts:
        heights = jnp.exp(jax.random.uniform(jax.random.fold_in(own, dim), (blocks,), jnp.float32, smallest / len(cuts), high / len(cuts)))
        loudness = loudness * jnp.repeat(heights, dims[dim] // blocks).reshape([-1 if axis == dim else 1 for axis in range(len(dims))])
    return loudness


def normal_values(stream_key, dims, spread, limit, pieces=(), dtype=jnp.bfloat16):
    loudness = levels(stream_key, dims, pieces, -0.22, 0.18) if pieces else 1.0
    values = jax.random.normal(stream_key, dims, jnp.float32) * spread * loudness
    return jnp.minimum(jnp.maximum(values, -limit), limit).astype(dtype)


def setup_inputs(seed: int = 0) -> dict:
    key_list = jax.random.split(jax.random.key(seed), 7)
    return {
        "grad_out": normal_values(key_list[0], (TOKENS, D), 0.5, 3.0, ((0, 128),)),
        "routes": draw_routes(jax.random.fold_in(key_list[6], 71), 0),
        "probs": jnp.clip(jnp.exp(math.log(0.5) - 3.224016 * jax.random.uniform(key_list[2], (TOKENS, TOP), jnp.float32) ** levels(key_list[2], (TOKENS, TOP), ((0, 128),), -0.2, 0.2)), 0.019897461, 0.5).astype(jnp.bfloat16),
        "hidden_act": normal_values(key_list[3], (TOKENS, TOP, FFW), 0.25, 1.5, ((0, 128),)),
        "placement": draw_placement(jax.random.fold_in(key_list[6], 71), 0),
        "down_weight": normal_values(key_list[5], (EXPERTS, FFW, D), FFW ** -0.5, 0.21875, ((0, 32),)),
    }


def reference(grad_out, routes, probs, hidden_act, placement, down_weight):
    tokens = grad_out.shape[0]
    route_rows = tokens * TOP
    expert = routes.reshape(route_rows).astype(jnp.int32)
    token_of = (jnp.arange(route_rows) // TOP).astype(jnp.int32)
    home_group = (token_of // (TOK_DEV * N_SP)).astype(jnp.int32)
    prob_rows = probs.reshape(route_rows)
    act_all = hidden_act.reshape(route_rows, FFW)
    seg_key = (expert * N_GRP + home_group).astype(jnp.int32)
    ordering = jnp.argsort(seg_key, stable=True).astype(jnp.int32)
    seg_count = jnp.zeros((EXPERTS * N_GRP,), jnp.int32).at[seg_key].add(1)
    seg_start = (jnp.cumsum(seg_count) - seg_count).astype(jnp.int32)
    seg_span = N_SP * MOST
    order_pad = jnp.concatenate([ordering, jnp.zeros((seg_span,), jnp.int32)])

    def per_expert(expert_id):
        weight = down_weight[expert_id]
        group_parts = []
        proj_list = []
        index_list = []
        for source in range(N_GRP):
            seg = expert_id * N_GRP + source
            start = seg_start[seg]
            row_index = lax.dynamic_slice_in_dim(order_pad, start, seg_span).astype(jnp.int32)
            is_live = jnp.arange(seg_span) < seg_count[seg]
            cotangent = grad_out[row_index // TOP]
            weights_now = jnp.where(is_live, prob_rows[row_index].astype(jnp.float32), 0.0)
            scaled = (weights_now[:, None] * cotangent.astype(jnp.float32)).astype(jnp.bfloat16)
            act_rows = act_all[row_index]
            group_parts.append(jnp.dot(act_rows.T, scaled, preferred_element_type=jnp.float32))
            projected = lax.dot_general(cotangent, weight, (((1,), (1,)), ((), ())), preferred_element_type=jnp.float32)
            proj_list.append(projected.astype(jnp.bfloat16))
            index_list.append(jnp.where(is_live, row_index, route_rows).astype(jnp.int32))
        holders = lax.dynamic_index_in_dim(placement, expert_id // 2, 1, keepdims=False) == expert_id
        lowest = jnp.argmax(holders).astype(jnp.int32)
        summed = jnp.zeros((FFW, D), jnp.float32)
        for replica in range(N_GRP):
            accum = jnp.zeros((FFW, D), jnp.float32)
            for source in range(N_GRP):
                serving = jnp.where(holders[source], source, lowest)
                accum = accum + jnp.where(serving == replica, group_parts[source], 0.0)
            rounded = lax.optimization_barrier(accum.astype(jnp.bfloat16))
            summed = summed + jnp.where(holders[replica], rounded.astype(jnp.float32), 0.0)
        return summed.astype(jnp.bfloat16), jnp.stack(proj_list), jnp.stack(index_list)

    grads_all, proj_rows, proj_index = lax.map(per_expert, jnp.arange(EXPERTS).astype(jnp.int32))
    proj_grad = jnp.zeros((route_rows, FFW), jnp.bfloat16).at[proj_index.reshape(-1)].set(
        proj_rows.reshape(-1, FFW), mode="drop")
    grad_act = (prob_rows.astype(jnp.float32)[:, None] * proj_grad.astype(jnp.float32)).astype(jnp.bfloat16)
    grad_prob = jnp.sum(act_all.astype(jnp.float32) * proj_grad.astype(jnp.float32), axis=-1)
    weight_grad = grads_all[placement]
    return grad_act.reshape(tokens, TOP, FFW), grad_prob.reshape(tokens, TOP), weight_grad
```

```python
import jax
import jax.numpy as jnp
from jax import lax
from jax.sharding import PartitionSpec as P

CHUNKS = 4


def shards(grad_out, routes, probs, hidden_act, placement, down_weight):
    grp_size = lax.axis_size("grp")
    sp_size = lax.axis_size("sp")
    my_group = lax.axis_index("grp")
    my_column = lax.axis_index("sp")
    tok, width = grad_out.shape
    top = routes.shape[1]
    hidden = hidden_act.shape[2]
    experts = 2 * sp_size
    base = tok * top // experts
    rows = 40
    slots = sp_size * rows
    bf16, f32 = jnp.bfloat16, jnp.float32

    hit = routes[:, :, None] == jnp.arange(experts)[None, None, :]
    member = jnp.any(hit, axis=1).astype(bf16)
    lower = (jnp.arange(tok)[:, None] > jnp.arange(tok)[None, :]).astype(bf16)
    rank = jnp.dot(lower, member, preferred_element_type=f32)
    route_rank = jnp.sum(jnp.where(hit, rank[:, None, :], 0.0), axis=2).astype(jnp.int32)
    low = routes % 2
    inner = jnp.where(route_rank < base, low * base + route_rank, 2 * base + low)
    slot = (routes // 2) * rows + inner
    ids = jnp.arange(slots)
    pick = jnp.any(ids[:, None, None] == slot[None, :, :], axis=2).astype(bf16)
    flat = slot.reshape(tok * top)
    onehot = ids[:, None] == flat[None, :]
    pick_act = jnp.where(onehot, probs.reshape(1, tok * top), 0).astype(bf16)
    act2 = hidden_act.reshape(tok * top, hidden)

    def exchange(v):
        return lax.all_to_all(v.reshape(sp_size, rows, v.shape[-1]), "sp", 0, 0, tiled=True)

    send_act = jnp.dot(pick_act, act2, preferred_element_type=f32).astype(bf16)
    got_act = exchange(send_act).reshape(sp_size, rows, hidden)
    step = width // CHUNKS
    got = []
    for c in range(CHUNKS):
        piece = jnp.dot(pick, grad_out[:, c * step : (c + 1) * step], preferred_element_type=f32).astype(bf16)
        got.append(exchange(piece).reshape(slots, step))

    kind = jnp.arange(rows)
    is_low = (kind < base) | (kind == 2 * base)
    is_high = ((kind >= base) & (kind < 2 * base)) | (kind == 2 * base + 1)
    act_low = jnp.where(is_low[None, :, None], got_act, 0).reshape(slots, hidden)
    act_high = jnp.where(is_high[None, :, None], got_act, 0).reshape(slots, hidden)
    quarter = hidden // grp_size
    held = lax.dynamic_index_in_dim(placement, my_column, 1, keepdims=False) - 2 * my_column
    outs = []
    for c in range(CHUNKS):
        parts = [
            lax.dot_general(a, got[c], (((0,), (0,)), ((), ())), preferred_element_type=f32)
            .astype(bf16)
            .reshape(grp_size, quarter, step)
            for a in (act_low, act_high)
        ]
        part = jnp.stack(parts, axis=1).reshape(grp_size * 2 * quarter, step)
        mine = lax.psum_scatter(part, "grp", scatter_dimension=0, tiled=True).reshape(2, quarter, step)
        wanted = jnp.where((held == 0)[:, None, None], mine[0][None], mine[1][None])
        outs.append(
            lax.all_to_all(wanted, "grp", 0, 0, tiled=True).reshape(hidden, step)
        )
    own = jnp.concatenate(outs, axis=1)

    proj = [
        sum(
            lax.dot_general(
                got[c], down_weight[j, :, c * step : (c + 1) * step], (((1,), (1,)), ((), ())),
                preferred_element_type=f32,
            )
            for c in range(CHUNKS)
        ).astype(bf16).reshape(sp_size, rows, hidden)
        for j in range(2)
    ]
    both = jnp.where(is_low[None, :, None], proj[0], jnp.where(is_high[None, :, None], proj[1], 0))
    back = exchange(both.reshape(slots, hidden)).reshape(slots, hidden)
    proj_rows = jnp.dot(onehot.astype(bf16).T, back, preferred_element_type=f32)
    prob_rows = probs.reshape(tok * top).astype(f32)
    grad_act = (prob_rows[:, None] * proj_rows).astype(bf16)
    grad_prob = jnp.sum(act2.astype(f32) * proj_rows, axis=-1)
    return (
        grad_act.reshape(tok, top, hidden),
        grad_prob.reshape(tok, top),
        own.reshape(1, 1, hidden, width),
    )


def solution(mesh):
    placed = (
        P(("grp", "sp"), None),
        P(("grp", "sp"), None),
        P(("grp", "sp"), None),
        P(("grp", "sp"), None, None),
        P(),
        P("sp", None, None),
    )
    return jax.shard_map(
        shards,
        mesh=mesh,
        in_specs=placed,
        out_specs=(
            P(("grp", "sp"), None, None),
            P(("grp", "sp"), None),
            P("grp", "sp", None, None),
        ),
        check_vma=False,
    )
```

```python
import jax
import jax.numpy as jnp
from jax import lax
from jax.sharding import PartitionSpec as P

PIECES = (1, 1, 2, 2, 2)


def tie(first, second):
    return lax.optimization_barrier((first, second))


def shards(grad_out, routes, probs, hidden_act, placement, down_weight):
    grp_size = lax.axis_size("grp")
    sp_size = lax.axis_size("sp")
    my_group = lax.axis_index("grp")
    my_column = lax.axis_index("sp")
    tok, width = grad_out.shape
    top = routes.shape[1]
    hidden = hidden_act.shape[2]
    experts = 2 * sp_size
    base = tok * top // experts
    rows = 40
    slots = sp_size * rows
    quarter = hidden // grp_size
    bf16, f32 = jnp.bfloat16, jnp.float32
    unit = width // 8
    spans, at = [], 0
    for p in PIECES:
        spans.append((at, at + p * unit))
        at += p * unit
    last = len(spans) - 1

    hit = routes[:, :, None] == jnp.arange(experts)[None, None, :]
    member = jnp.any(hit, axis=1).astype(bf16)
    lower = (jnp.arange(tok)[:, None] > jnp.arange(tok)[None, :]).astype(bf16)
    rank = jnp.dot(lower, member, preferred_element_type=f32)
    route_rank = jnp.sum(jnp.where(hit, rank[:, None, :], 0.0), axis=2).astype(jnp.int32)
    low = routes % 2
    inner = jnp.where(route_rank < base, low * base + route_rank, 2 * base + low)
    slot = (routes // 2) * rows + inner
    ids = jnp.arange(slots)
    pick = jnp.any(ids[:, None, None] == slot[None, :, :], axis=2).astype(bf16)
    flat = slot.reshape(tok * top)
    onehot = ids[:, None] == flat[None, :]
    pick_act = jnp.where(onehot, probs.reshape(1, tok * top), 0).astype(bf16)
    act2 = hidden_act.reshape(tok * top, hidden)

    def exchange(v):
        got = lax.all_to_all(v.reshape(sp_size, rows, v.shape[-1]), "sp", 0, 0, tiled=True)
        return got.reshape(slots, v.shape[-1])

    def piece(c):
        return jnp.dot(pick, grad_out[:, spans[c][0] : spans[c][1]], preferred_element_type=f32).astype(bf16)

    kind = jnp.arange(slots) % rows
    is_low = (kind < base) | (kind == 2 * base)
    is_high = ((kind >= base) & (kind < 2 * base)) | (kind == 2 * base + 1)
    held = lax.dynamic_index_in_dim(placement, my_column, 1, keepdims=False) - 2 * my_column
    steps = [[(i, (i + d) % grp_size) for i in range(grp_size)] for d in range(grp_size)]

    def partial_sums(got):
        parts = [
            lax.dot_general(a, got, (((0,), (0,)), ((), ())), preferred_element_type=f32)
            .astype(bf16)
            .reshape(grp_size, quarter, got.shape[1])
            for a in acts
        ]
        part = jnp.stack(parts, axis=1).reshape(grp_size * 2 * quarter, got.shape[1])
        return lax.psum_scatter(part, "grp", scatter_dimension=0, tiled=True).reshape(2, quarter, got.shape[1])

    def wanted(mine):
        out = []
        for d in range(grp_size):
            which = lax.dynamic_index_in_dim(held, (my_group + d) % grp_size, 0, keepdims=False)
            out.append(jnp.where(which == 0, mine[0], mine[1]))
        return out

    def project(got, c):
        w = down_weight[:, :, spans[c][0] : spans[c][1]]
        dims = (((1,), (1,)), ((), ()))
        lowp = lax.dot_general(got, w[0], dims, preferred_element_type=f32)
        highp = lax.dot_general(got, w[1], dims, preferred_element_type=f32)
        return jnp.where(is_low[:, None], lowp, highp)

    own = jnp.zeros((hidden, width), bf16)

    def place(own, sends, c):
        for d in range(grp_size):
            block = lax.ppermute(sends[d], "grp", steps[d]) if d else sends[d]
            source = (my_group + grp_size - d) % grp_size
            own = lax.dynamic_update_slice(own, block, (source * quarter, spans[c][0]))
        return own

    send_act = jnp.dot(pick_act, act2, preferred_element_type=f32).astype(bf16)
    first = exchange(jnp.concatenate([send_act, piece(0)], axis=1))
    got_act = first[:, :hidden]
    acts = [jnp.where(m[:, None], got_act, 0) for m in (is_low, is_high)]
    got = first[:, hidden:]
    mine = {}
    total = None
    sends = {}
    for c in range(last + 1):
        mine[c] = partial_sums(got)
        if c < last:
            out = piece(c + 1)
            if total is not None:
                out, total = tie(out, total)
            if c in (1, 2):
                out, sends[c - 1] = tie(out, wanted(mine[c - 1]))
            nxt = exchange(out)
        else:
            got, sends[c - 2] = tie(got, wanted(mine[c - 2]))
        here = project(got, c)
        total = here if total is None else total + here
        if c < last:
            got = nxt
    proj = jnp.where((is_low | is_high)[:, None], total, 0).astype(bf16)
    proj, sends[last - 1] = tie(proj, wanted(mine[last - 1]))
    back = exchange(proj)
    sends[last] = wanted(mine[last])
    for c in range(last + 1):
        own = place(own, sends[c], c)

    proj_rows = jnp.dot(onehot.astype(bf16).T, back, preferred_element_type=f32)
    prob_rows = probs.reshape(tok * top).astype(f32)
    grad_act = (prob_rows[:, None] * proj_rows).astype(bf16)
    grad_prob = jnp.sum(act2.astype(f32) * proj_rows, axis=-1)
    return (
        grad_act.reshape(tok, top, hidden),
        grad_prob.reshape(tok, top),
        own.reshape(1, 1, hidden, width),
    )


def solution(mesh):
    placed = (
        P(("grp", "sp"), None),
        P(("grp", "sp"), None),
        P(("grp", "sp"), None),
        P(("grp", "sp"), None, None),
        P(),
        P("sp", None, None),
    )
    return jax.shard_map(
        shards,
        mesh=mesh,
        in_specs=placed,
        out_specs=(
            P(("grp", "sp"), None, None),
            P(("grp", "sp"), None),
            P("grp", "sp", None, None),
        ),
        check_vma=False,
    )
```

```python
import functools

import jax
import jax.numpy as jnp
from jax import lax
from jax.experimental import pallas as pl
from jax.experimental.pallas import tpu as pltpu
from jax.sharding import PartitionSpec as P

V = 256
MAIN = 32
TAIL = 8
SHIFT = 6
MASK = (1 << SHIFT) - 1
CHUNKS = (1, 3, 4, 4, 4)
BF16 = jnp.bfloat16
F32 = jnp.float32
VMEM = 48 * 1024 * 1024


def tie(first, second):
    return lax.optimization_barrier((first, second))


def dot(a, b, dims=((1,), (0,))):
    return lax.dot_general(a, b, (dims, ((), ())), preferred_element_type=F32)


def cost(flops, bytes_accessed):
    return pl.CostEstimate(flops=int(flops), bytes_accessed=int(bytes_accessed), transcendentals=0)


def params():
    return pltpu.CompilerParams(vmem_limit_bytes=VMEM)


def whole(shape):
    return pl.BlockSpec(shape, lambda *_: (0,) * len(shape))


def block_rows(n):
    return MAIN * n + TAIL


SEND_STEP = 8


def main_ids(first, rows):
    i = lax.broadcasted_iota(jnp.int32, (rows, 1), 0)
    return ((first + i // MAIN) << SHIFT) + i % MAIN


def tail_ids(first, part):
    i = lax.broadcasted_iota(jnp.int32, (SEND_STEP * TAIL, 1), 0)
    r = i % TAIL
    return jnp.where(r // 2 == part, ((first + i // TAIL) << SHIFT) + MAIN + r % 2, -1)


def hits(ids, codes):
    found = ids == codes[0:1, :]
    for k in range(1, codes.shape[0]):
        found = found | (ids == codes[k : k + 1, :])
    return jnp.where(found, 1.0, 0.0).astype(BF16)


def store_main(out_ref, part, values):
    out_ref[:, part * MAIN : (part + 1) * MAIN, :] = values.astype(BF16).reshape(SEND_STEP, MAIN, V)


def send_first_kernel(codes_ref, flat_ref, prob_ref, act_ref, grad_ref, out_ref):
    first = pl.program_id(0) * SEND_STEP
    codes, flat, prob = codes_ref[...], flat_ref[...], prob_ref[...]
    ids = main_ids(first, SEND_STEP * MAIN)
    pick = jnp.where(ids == flat, prob, 0.0).astype(BF16)
    act_parts = act_ref.shape[1] // V
    tail = jnp.zeros((SEND_STEP * TAIL, V), F32)
    for p in range(act_parts):
        act = act_ref[:, p * V : (p + 1) * V]
        store_main(out_ref, p, dot(pick, act))
        tail += dot(jnp.where(tail_ids(first, p) == flat, prob, 0.0).astype(BF16), act)
    grad = grad_ref[...]
    grads = hits(ids, codes)
    for p in range(grad.shape[1] // V):
        part = grad[:, p * V : (p + 1) * V]
        store_main(out_ref, act_parts + p, dot(grads, part))
        tail += dot(hits(tail_ids(first, act_parts + p), codes), part)
    out_ref[:, out_ref.shape[1] - TAIL :, :] = tail.astype(BF16).reshape(SEND_STEP, TAIL, V)


def send_kernel(chunks, codes_ref, grad_ref, *out_refs):
    first = pl.program_id(0) * SEND_STEP
    codes = codes_ref[...]
    grads = hits(main_ids(first, SEND_STEP * MAIN), codes)
    at = 0
    for n, out_ref in zip(chunks, out_refs):
        tail = jnp.zeros((SEND_STEP * TAIL, V), F32)
        for p in range(n):
            part = grad_ref[:, at : at + V]
            store_main(out_ref, p, dot(grads, part))
            tail += dot(hits(tail_ids(first, p), codes), part)
            at += V
        out_ref[:, MAIN * n :, :] = tail.astype(BF16).reshape(SEND_STEP, TAIL, V)


def send_first(codes, flat, prob, act, grad, columns, parts):
    routes, hidden = act.shape
    tok = grad.shape[0]
    rows = block_rows(hidden // V + parts)
    return pl.pallas_call(
        send_first_kernel,
        grid=(columns // SEND_STEP,),
        in_specs=[
            whole(codes.shape),
            whole(flat.shape),
            whole(prob.shape),
            whole(act.shape),
            pl.BlockSpec((tok, parts * V), lambda i: (0, 0)),
        ],
        out_specs=pl.BlockSpec((SEND_STEP, rows, V), lambda i: (i, 0, 0)),
        out_shape=jax.ShapeDtypeStruct((columns, rows, V), BF16),
        compiler_params=params(),
        cost_estimate=cost(2 * columns * MAIN * routes * hidden, 2 * columns * rows * V + 2 * routes * hidden),
        name="send_first",
    )(codes, flat, prob, act, grad)


def send_rest(codes, grad, columns, chunks):
    tok, width = grad.shape
    shapes = [(columns, block_rows(n), V) for n in chunks]
    return pl.pallas_call(
        functools.partial(send_kernel, chunks),
        grid=(columns // SEND_STEP,),
        in_specs=[whole(codes.shape), whole(grad.shape)],
        out_specs=[pl.BlockSpec((SEND_STEP, s[1], V), lambda i: (i, 0, 0)) for s in shapes],
        out_shape=[jax.ShapeDtypeStruct(s, BF16) for s in shapes],
        compiler_params=params(),
        cost_estimate=cost(2 * columns * MAIN * tok * width, 2 * columns * 34 * width + 2 * tok * width),
        name="send_rest",
    )(codes, grad)


def sorted_tail(got_ref):
    sources = got_ref.shape[0]
    tail = got_ref[:, got_ref.shape[1] - TAIL :, :].astype(F32).reshape(sources * TAIL, V).astype(BF16)
    size = sources * TAIL
    i = lax.broadcasted_iota(jnp.int32, (size, size), 0)
    j = lax.broadcasted_iota(jnp.int32, (size, size), 1)
    order = (i % sources == j // TAIL) & (i // sources == j % TAIL)
    return dot(jnp.where(order, 1.0, 0.0).astype(BF16), tail).astype(BF16)


def main_rows(got_ref, part, expert):
    half = MAIN // 2
    rows = got_ref[:, pl.ds(part * MAIN + expert * half, half), :]
    return rows.reshape(got_ref.shape[0] * half, V)


def tail_rows(tail, sources, part, expert):
    at = (2 * part + expert) * sources
    return tail[at : at + sources, :]


def weight_step(acts, rows, more, out_ref, expert):
    depth = rows.shape[0]
    total = dot(acts[:, :depth], rows) + dot(acts[:, depth:], more)
    quarters, _, size, _ = out_ref.shape
    for q in range(quarters):
        out_ref[q, expert] = total[q * size : (q + 1) * size].astype(BF16)


def weight_first_kernel(act_parts, got_ref, acts_ref, out_ref):
    sources = got_ref.shape[0]
    tail = sorted_tail(got_ref)
    for e in range(2):
        for p in range(act_parts):
            block = main_rows(got_ref, p, e)
            more = tail_rows(tail, sources, p, e)
            acts_ref[e, p * V : (p + 1) * V, : block.shape[0]] = block.astype(F32).T.astype(BF16)
            acts_ref[e, p * V : (p + 1) * V, block.shape[0] :] = more.astype(F32).T.astype(BF16)
        weight_step(
            acts_ref[e], main_rows(got_ref, act_parts, e), tail_rows(tail, sources, act_parts, e), out_ref, e
        )


def weight_kernel(parts, acts_ref, got_ref, out_ref, tail_ref):
    sources = got_ref.shape[0]
    part = pl.program_id(0)

    @pl.when(part == 0)
    def _():
        tail_ref[...] = sorted_tail(got_ref)

    for e in range(2):
        more = tail_ref[pl.ds(pl.multiple_of((2 * part + e) * sources, sources), sources), :]
        weight_step(acts_ref[e], main_rows(got_ref, part, e), more, out_ref, e)


def weight_first(got, hidden, groups):
    sources = got.shape[0]
    depth = sources * (MAIN // 2 + 1)
    return pl.pallas_call(
        functools.partial(weight_first_kernel, hidden // V),
        grid=(1,),
        in_specs=[whole(got.shape)],
        out_specs=[whole((2, hidden, depth)), whole((groups, 2, hidden // groups, V))],
        out_shape=[
            jax.ShapeDtypeStruct((2, hidden, depth), BF16),
            jax.ShapeDtypeStruct((groups, 2, hidden // groups, V), BF16),
        ],
        compiler_params=params(),
        cost_estimate=cost(4 * depth * hidden * V, 2 * (got.size + 4 * depth * hidden)),
        name="weight_first",
    )(got)


def weight_rest(acts, got, parts, groups):
    hidden, depth = acts.shape[1:]
    return pl.pallas_call(
        functools.partial(weight_kernel, parts),
        grid=(parts,),
        in_specs=[whole(acts.shape), whole(got.shape)],
        out_specs=pl.BlockSpec((groups, 2, hidden // groups, V), lambda p: (0, 0, 0, p)),
        out_shape=jax.ShapeDtypeStruct((groups, 2, hidden // groups, parts * V), BF16),
        scratch_shapes=[pltpu.VMEM((got.shape[0] * TAIL, V), BF16)],
        compiler_params=params(),
        cost_estimate=cost(4 * depth * hidden * V * parts, 2 * (got.size + acts.size + 2 * hidden * V * parts)),
        name="weight_rest",
    )(acts, got)


def project_kernel(skip, parts, chained, final, *refs):
    refs = list(refs)
    got_ref, weight_ref = refs[:2]
    refs = refs[2:]
    if chained:
        main_in, tail_in = refs[:2]
        refs = refs[2:]
    if final:
        out_ref, main_acc, tail_acc, tail_ref = refs
    else:
        main_acc, tail_acc, tail_ref = refs
    sources = got_ref.shape[0]
    half = MAIN // 2
    part = pl.program_id(0)

    @pl.when(part == 0)
    def _():
        tail_ref[...] = sorted_tail(got_ref)
        if chained:
            main_acc[...] = main_in[...]
            tail_acc[...] = tail_in[...]
        else:
            main_acc[...] = jnp.zeros_like(main_acc)
            tail_acc[...] = jnp.zeros_like(tail_acc)

    for e in range(2):
        weight = weight_ref[e]
        rows = main_rows(got_ref, part + skip, e)
        main_acc[e] += dot(rows, weight, ((1,), (1,)))
        more = tail_ref[pl.ds(pl.multiple_of((2 * (part + skip) + e) * sources, sources), sources), :]
        tail_acc[e] += dot(more, weight, ((1,), (1,)))

    if final:

        @pl.when(part == parts - 1)
        def _():
            hidden = weight_ref.shape[1]
            n = hidden // V
            size = sources * TAIL
            i = lax.broadcasted_iota(jnp.int32, (size, sources), 0)
            j = lax.broadcasted_iota(jnp.int32, (size, sources), 1)
            tail = jnp.zeros((size, V), F32)
            for e in range(2):
                for p in range(n):
                    block = main_acc[e, :, p * V : (p + 1) * V].astype(BF16)
                    at = p * MAIN + e * half
                    out_ref[:, at : at + half, :] = block.reshape(sources, half, V)
                    order = (i // TAIL == j) & (i % TAIL == 2 * p + e)
                    more = tail_acc[e, :, p * V : (p + 1) * V].astype(BF16)
                    tail += dot(jnp.where(order, 1.0, 0.0).astype(BF16), more)
            out_ref[:, n * MAIN :, :] = tail.reshape(sources, TAIL, V).astype(BF16)


def project(got, weight, at, skip, parts, state, final):
    sources = got.shape[0]
    hidden = weight.shape[1]
    half = MAIN // 2
    main_shape, tail_shape = (2, sources * half, hidden), (2, sources, hidden)
    in_specs = [whole(got.shape), pl.BlockSpec((2, hidden, V), lambda p: (0, 0, at + p))]
    args = [got, weight]
    if state is not None:
        in_specs += [whole(main_shape), whole(tail_shape)]
        args += list(state)
    scratch = [pltpu.VMEM((sources * TAIL, V), BF16)]
    if final:
        shape = (sources, block_rows(hidden // V), V)
        out_specs, out_shape = whole(shape), jax.ShapeDtypeStruct(shape, BF16)
        scratch = [pltpu.VMEM(main_shape, F32), pltpu.VMEM(tail_shape, F32)] + scratch
    else:
        out_specs = [whole(main_shape), whole(tail_shape)]
        out_shape = [jax.ShapeDtypeStruct(main_shape, F32), jax.ShapeDtypeStruct(tail_shape, F32)]
    return pl.pallas_call(
        functools.partial(project_kernel, skip, parts, state is not None, final),
        grid=(parts,),
        in_specs=in_specs,
        out_specs=out_specs,
        out_shape=out_shape,
        scratch_shapes=scratch,
        compiler_params=params(),
        cost_estimate=cost(4 * sources * 17 * hidden * V * parts, 2 * got.size + 4 * hidden * V * parts + 16 * sources * 17 * hidden),
        name="project",
    )(*args)


FINISH_STEP = 256


def finish_kernel(code_ref, prob_ref, act_ref, back_ref, grad_act_ref, grad_prob_ref):
    code = code_ref[...]
    column, row = code >> SHIFT, code & MASK
    sources = back_ref.shape[0]
    hidden = act_ref.shape[1]
    n = hidden // V
    steps = code.shape[0]
    main_id = jnp.where(row < MAIN, column * MAIN + row, -1)
    lanes = lax.broadcasted_iota(jnp.int32, (steps, sources * MAIN), 1)
    pick = jnp.where(lanes == main_id, 1.0, 0.0).astype(BF16)
    tail = back_ref[:, n * MAIN :, :].astype(F32).reshape(sources * TAIL, V).astype(BF16)
    lanes = lax.broadcasted_iota(jnp.int32, (steps, sources * TAIL), 1)
    prob = prob_ref[...]
    total = jnp.zeros((steps, 1), F32)
    for p in range(n):
        main = back_ref[:, p * MAIN : (p + 1) * MAIN, :].reshape(sources * MAIN, V)
        tail_id = jnp.where(row >= MAIN, column * TAIL + 2 * p + (row - MAIN), -1)
        proj = dot(pick, main) + dot(jnp.where(lanes == tail_id, 1.0, 0.0).astype(BF16), tail)
        act = act_ref[:, p * V : (p + 1) * V].astype(F32)
        total += jnp.sum(act * proj, axis=1, keepdims=True)
        grad_act_ref[:, p * V : (p + 1) * V] = (prob * proj).astype(BF16)
    grad_prob_ref[...] = total


def finish(code, prob, act, back):
    routes, hidden = act.shape
    one = pl.BlockSpec((FINISH_STEP, 1), lambda i: (i, 0))
    rows = pl.BlockSpec((FINISH_STEP, hidden), lambda i: (i, 0))
    return pl.pallas_call(
        finish_kernel,
        grid=(routes // FINISH_STEP,),
        in_specs=[one, one, rows, whole(back.shape)],
        out_specs=[rows, one],
        out_shape=[jax.ShapeDtypeStruct((routes, hidden), BF16), jax.ShapeDtypeStruct((routes, 1), F32)],
        compiler_params=params(),
        cost_estimate=cost(2 * routes * routes * hidden, 2 * (back.size + 2 * routes * hidden)),
        name="finish",
    )(code, prob, act, back)


def route_codes(routes, columns):
    tok, top = routes.shape
    experts = 2 * columns
    base = MAIN // 2
    hit = routes[:, :, None] == jnp.arange(experts)[None, None, :]
    member = jnp.any(hit, axis=1).astype(BF16)
    lower = (jnp.arange(tok)[:, None] > jnp.arange(tok)[None, :]).astype(BF16)
    rank = dot(lower, member)
    rank = jnp.sum(jnp.where(hit, rank[:, None, :], 0.0), axis=2).astype(jnp.int32)
    low = routes % 2
    row = jnp.where(rank < base, low * base + rank, MAIN + low)
    return ((routes // 2) << SHIFT) + row


def shards(grad_out, routes, probs, hidden_act, placement, down_weight):
    groups = lax.axis_size("grp")
    columns = lax.axis_size("sp")
    my_group = lax.axis_index("grp")
    my_column = lax.axis_index("sp")
    tok, width = grad_out.shape
    top = routes.shape[1]
    hidden = hidden_act.shape[2]
    quarter = hidden // groups
    act_parts = hidden // V
    last = len(CHUNKS) - 1

    codes = route_codes(routes, columns)
    flat = codes.reshape(1, tok * top)
    prob = probs.astype(F32)
    act = hidden_act.reshape(tok * top, hidden)

    def exchange(v):
        return lax.all_to_all(v, "sp", 0, 0, tiled=True)

    held = lax.dynamic_index_in_dim(placement, my_column, 1, keepdims=False) - 2 * my_column
    hops = [[(i, (i + d) % groups) for i in range(groups)] for d in range(groups)]

    def reduced(part):
        size = part.shape[-1]
        flat_part = part.reshape(groups * 2 * quarter, size)
        return lax.psum_scatter(flat_part, "grp", scatter_dimension=0, tiled=True).reshape(2, quarter, size)

    def wanted(mine):
        out = []
        for d in range(groups):
            which = lax.dynamic_index_in_dim(held, (my_group + d) % groups, 0, keepdims=False)
            out.append(jnp.where(which == 0, mine[0], mine[1]))
        return out

    own = jnp.zeros((hidden, width), BF16)

    def moved(sends):
        return [lax.ppermute(sends[d], "grp", hops[d]) if d else sends[d] for d in range(groups)]

    def place(own, blocks, at):
        for d in range(groups):
            source = (my_group + groups - d) % groups
            own = lax.dynamic_update_slice(own, blocks[d], (source * quarter, at))
        return own

    codes_t = codes.T
    first = send_first(codes_t, flat, prob.reshape(1, tok * top), act, grad_out, columns, CHUNKS[0])
    got = {0: exchange(first)}
    outs = send_rest(codes_t, grad_out[:, CHUNKS[0] * V :], columns, CHUNKS[1:])
    outs = dict(enumerate(outs, 1))

    starts = [sum(CHUNKS[:c]) for c in range(last + 1)]
    mine, sends, blocks = {}, {}, {}
    state = None
    acts, part = weight_first(got[0], hidden, groups)
    for c in range(last + 1):
        if c:
            if c == last:
                got[c], state = tie(got[c], state)
            if c >= 2:
                got[c], blocks[c - 2] = tie(got[c], moved(sends[c - 2]))
            part = weight_rest(acts, got[c], CHUNKS[c], groups)
        mine[c] = reduced(part)
        if c < last:
            if c >= 1:
                outs[c + 1], sends[c - 1] = tie(outs[c + 1], wanted(mine[c - 1]))
            got[c + 1] = exchange(outs[c + 1])
            skip = act_parts if c == 0 else 0
            state = project(got[c], down_weight, starts[c], skip, CHUNKS[c], state, False)
    proj = project(got[last], down_weight, starts[last], 0, CHUNKS[last], state, True)
    proj, sends[last - 1] = tie(proj, wanted(mine[last - 1]))
    back = exchange(proj)
    sends[last] = wanted(mine[last])
    for c in range(last + 1):
        own = place(own, blocks[c] if c in blocks else moved(sends[c]), starts[c] * V)

    grad_act, grad_prob = finish(codes.reshape(tok * top, 1), prob.reshape(tok * top, 1), act, back)
    return (
        grad_act.reshape(tok, top, hidden),
        grad_prob.reshape(tok, top),
        own.reshape(1, 1, hidden, width),
    )


def solution(mesh):
    placed = (
        P(("grp", "sp"), None),
        P(("grp", "sp"), None),
        P(("grp", "sp"), None),
        P(("grp", "sp"), None, None),
        P(),
        P("sp", None, None),
    )
    return jax.shard_map(
        shards,
        mesh=mesh,
        in_specs=placed,
        out_specs=(
            P(("grp", "sp"), None, None),
            P(("grp", "sp"), None),
            P("grp", "sp", None, None),
        ),
        check_vma=False,
    )
```

```python
import functools

import jax
import jax.numpy as jnp
from jax import lax
from jax.experimental import pallas as pl
from jax.experimental.pallas import tpu as pltpu
from jax.sharding import PartitionSpec as P

V = 256
MAIN = 32
SHIFT = 6
MASK = (1 << SHIFT) - 1
CHUNKS = (5, 6, 5)
BF16 = jnp.bfloat16
F32 = jnp.float32
MIB = 1024 * 1024


def tie(first, second):
    return lax.optimization_barrier((first, second))


def dot(a, b, dims=((1,), (0,))):
    return lax.dot_general(a, b, (dims, ((), ())), preferred_element_type=F32)


def cost(flops, bytes_accessed):
    return pl.CostEstimate(flops=int(flops), bytes_accessed=int(bytes_accessed), transcendentals=0)


def params(mib):
    return pltpu.CompilerParams(vmem_limit_bytes=mib * MIB)


def resident():
    return pl.BlockSpec(memory_space=pltpu.VMEM)


def in_hbm(x):
    return pltpu.with_memory_space_constraint(x, pltpu.HBM)


def whole(shape):
    return pl.BlockSpec(shape, lambda *_: (0,) * len(shape))


def tail_size(n):
    return (2 * n + 7) // 8 * 8


def block_rows(n):
    return MAIN * n + tail_size(n)


SEND_STEP = 8


def main_ids(first, rows):
    i = lax.broadcasted_iota(jnp.int32, (rows, 1), 0)
    return ((first + i // MAIN) << SHIFT) + i % MAIN


def tail_ids(first, size, part):
    i = lax.broadcasted_iota(jnp.int32, (SEND_STEP * size, 1), 0)
    r = i % size
    return jnp.where(r // 2 == part, ((first + i // size) << SHIFT) + MAIN + r % 2, -1)


def hits(ids, codes):
    found = ids == codes[0:1, :]
    for k in range(1, codes.shape[0]):
        found = found | (ids == codes[k : k + 1, :])
    return jnp.where(found, 1.0, 0.0).astype(BF16)


def store_main(out_ref, part, values):
    out_ref[:, part * MAIN : (part + 1) * MAIN, :] = values.astype(BF16).reshape(SEND_STEP, MAIN, V)


def send_first_kernel(codes_ref, flat_ref, prob_ref, act_ref, grad_ref, out_ref):
    first = pl.program_id(0) * SEND_STEP
    codes, flat, prob = codes_ref[...], flat_ref[...], prob_ref[...]
    ids = main_ids(first, SEND_STEP * MAIN)
    pick = jnp.where(ids == flat, prob, 0.0).astype(BF16)
    act_parts = act_ref.shape[1] // V
    grad = grad_ref[...]
    parts = grad.shape[1] // V
    size = tail_size(act_parts + parts)
    tail = jnp.zeros((SEND_STEP * size, V), F32)
    for p in range(act_parts):
        act = act_ref[:, p * V : (p + 1) * V]
        store_main(out_ref, p, dot(pick, act))
        tail += dot(jnp.where(tail_ids(first, size, p) == flat, prob, 0.0).astype(BF16), act)
    grads = hits(ids, codes)
    for p in range(parts):
        part = grad[:, p * V : (p + 1) * V]
        store_main(out_ref, act_parts + p, dot(grads, part))
        tail += dot(hits(tail_ids(first, size, act_parts + p), codes), part)
    out_ref[:, out_ref.shape[1] - size :, :] = tail.astype(BF16).reshape(SEND_STEP, size, V)


def send_kernel(start, chunks, codes_ref, grad_ref, *out_refs):
    first = pl.program_id(0) * SEND_STEP
    codes = codes_ref[...]
    grads = hits(main_ids(first, SEND_STEP * MAIN), codes)
    at = start * V
    for n, out_ref in zip(chunks, out_refs):
        size = tail_size(n)
        tail = jnp.zeros((SEND_STEP * size, V), F32)
        for p in range(n):
            part = grad_ref[:, at : at + V]
            store_main(out_ref, p, dot(grads, part))
            tail += dot(hits(tail_ids(first, size, p), codes), part)
            at += V
        out_ref[:, MAIN * n :, :] = tail.astype(BF16).reshape(SEND_STEP, size, V)


def send_first(codes, flat, prob, act, grad, columns, parts):
    routes, hidden = act.shape
    tok = grad.shape[0]
    rows = block_rows(hidden // V + parts)
    return pl.pallas_call(
        send_first_kernel,
        grid=(columns // SEND_STEP,),
        in_specs=[
            whole(codes.shape),
            whole(flat.shape),
            whole(prob.shape),
            whole(act.shape),
            pl.BlockSpec((tok, parts * V), lambda i: (0, 0)),
        ],
        out_specs=pl.BlockSpec((SEND_STEP, rows, V), lambda i: (i, 0, 0)),
        out_shape=jax.ShapeDtypeStruct((columns, rows, V), BF16),
        compiler_params=params(24),
        cost_estimate=cost(2 * columns * MAIN * routes * hidden, 2 * columns * rows * V + 2 * routes * hidden),
        name="send_first",
    )(codes, flat, prob, act, grad)


def send_rest(codes, grad, columns, start, chunks):
    tok, width = grad.shape
    shapes = [(columns, block_rows(n), V) for n in chunks]
    return pl.pallas_call(
        functools.partial(send_kernel, start, chunks),
        grid=(columns // SEND_STEP,),
        in_specs=[whole(codes.shape), whole(grad.shape)],
        out_specs=[pl.BlockSpec((SEND_STEP, s[1], V), lambda i: (i, 0, 0)) for s in shapes],
        out_shape=[jax.ShapeDtypeStruct(s, BF16) for s in shapes],
        compiler_params=params(24),
        cost_estimate=cost(2 * columns * MAIN * tok * width, 2 * columns * 34 * width + 2 * tok * width),
        name="send_rest",
    )(codes, grad)


def sorted_tail(got_ref):
    sources, rows, _ = got_ref.shape
    n = rows // MAIN
    tail = tail_size(n)
    size = sources * tail
    values = got_ref[:, n * MAIN :, :].astype(F32).reshape(size, V).astype(BF16)
    i = lax.broadcasted_iota(jnp.int32, (size, size), 0)
    j = lax.broadcasted_iota(jnp.int32, (size, size), 1)
    order = (i % sources == j // tail) & (i // sources == j % tail)
    return dot(jnp.where(order, 1.0, 0.0).astype(BF16), values).astype(BF16)


def main_rows(got_ref, part, expert):
    half = MAIN // 2
    rows = got_ref[:, pl.ds(part * MAIN + expert * half, half), :]
    return rows.reshape(got_ref.shape[0] * half, V)


def weight_step(acts, rows, more, out_ref, expert):
    depth = rows.shape[0]
    total = dot(acts[:, :depth], rows) + dot(acts[:, depth:], more)
    quarters, _, size, _ = out_ref.shape
    for q in range(quarters):
        out_ref[q, expert] = total[q * size : (q + 1) * size].astype(BF16)


def weight_first_kernel(act_parts, got_ref, acts_ref, out_ref, tail_ref):
    sources = got_ref.shape[0]
    part = pl.program_id(0)

    @pl.when(part == 0)
    def _():
        tail_ref[...] = sorted_tail(got_ref)
        for e in range(2):
            for p in range(act_parts):
                block = main_rows(got_ref, p, e)
                more = tail_ref[(2 * p + e) * sources : (2 * p + e + 1) * sources, :]
                acts_ref[e, p * V : (p + 1) * V, : block.shape[0]] = block.astype(F32).T.astype(BF16)
                acts_ref[e, p * V : (p + 1) * V, block.shape[0] :] = more.astype(F32).T.astype(BF16)

    for e in range(2):
        at = pl.multiple_of((2 * (act_parts + part) + e) * sources, sources)
        more = tail_ref[pl.ds(at, sources), :]
        weight_step(acts_ref[e], main_rows(got_ref, act_parts + part, e), more, out_ref, e)


def weight_kernel(parts, acts_ref, got_ref, out_ref, tail_ref):
    sources = got_ref.shape[0]
    part = pl.program_id(0)

    @pl.when(part == 0)
    def _():
        tail_ref[...] = sorted_tail(got_ref)

    for e in range(2):
        more = tail_ref[pl.ds(pl.multiple_of((2 * part + e) * sources, sources), sources), :]
        weight_step(acts_ref[e], main_rows(got_ref, part, e), more, out_ref, e)


def weight_first(got, hidden, parts, groups):
    sources = got.shape[0]
    depth = sources * (MAIN // 2 + 1)
    return pl.pallas_call(
        functools.partial(weight_first_kernel, hidden // V),
        grid=(parts,),
        in_specs=[resident()],
        out_specs=[
            whole((2, hidden, depth)),
            pl.BlockSpec((groups, 2, hidden // groups, V), lambda p: (0, 0, 0, p)),
        ],
        out_shape=[
            pltpu.HBM((2, hidden, depth), BF16),
            pltpu.HBM((groups, 2, hidden // groups, parts * V), BF16),
        ],
        scratch_shapes=[pltpu.VMEM((sources * (got.shape[1] % MAIN), V), BF16)],
        compiler_params=params(16),
        cost_estimate=cost(4 * depth * hidden * V * parts, 2 * (got.size + 4 * depth * hidden)),
        name="weight_first",
    )(got)


def weight_rest(acts, got, parts, groups):
    hidden, depth = acts.shape[1:]
    return pl.pallas_call(
        functools.partial(weight_kernel, parts),
        grid=(parts,),
        in_specs=[whole(acts.shape), resident()],
        out_specs=pl.BlockSpec((groups, 2, hidden // groups, V), lambda p: (0, 0, 0, p)),
        out_shape=pltpu.HBM((groups, 2, hidden // groups, parts * V), BF16),
        scratch_shapes=[pltpu.VMEM((got.shape[0] * (got.shape[1] % MAIN), V), BF16)],
        compiler_params=params(16),
        cost_estimate=cost(4 * depth * hidden * V * parts, 2 * (got.size + acts.size + 2 * hidden * V * parts)),
        name="weight_rest",
    )(in_hbm(acts), got)


def project_kernel(skip, parts, chained, final, *refs):
    refs = list(refs)
    got_ref, weight_ref = refs[:2]
    refs = refs[2:]
    if chained:
        main_in, tail_in = refs[:2]
        refs = refs[2:]
    if final:
        out_ref, main_acc, tail_acc, tail_ref = refs
    else:
        main_acc, tail_acc, tail_ref = refs
    sources = got_ref.shape[0]
    half = MAIN // 2
    part = pl.program_id(0)

    @pl.when(part == 0)
    def _():
        tail_ref[...] = sorted_tail(got_ref)
        if chained:
            main_acc[...] = main_in[...]
            tail_acc[...] = tail_in[...]
        else:
            main_acc[...] = jnp.zeros_like(main_acc)
            tail_acc[...] = jnp.zeros_like(tail_acc)

    for e in range(2):
        weight = weight_ref[e]
        rows = main_rows(got_ref, part + skip, e)
        main_acc[e] += dot(rows, weight, ((1,), (1,)))
        more = tail_ref[pl.ds(pl.multiple_of((2 * (part + skip) + e) * sources, sources), sources), :]
        tail_acc[e] += dot(more, weight, ((1,), (1,)))

    if final:

        @pl.when(part == parts - 1)
        def _():
            hidden = weight_ref.shape[1]
            n = hidden // V
            rows = tail_size(n)
            size = sources * rows
            i = lax.broadcasted_iota(jnp.int32, (size, sources), 0)
            j = lax.broadcasted_iota(jnp.int32, (size, sources), 1)
            tail = jnp.zeros((size, V), F32)
            for e in range(2):
                for p in range(n):
                    block = main_acc[e, :, p * V : (p + 1) * V].astype(BF16)
                    at = p * MAIN + e * half
                    out_ref[:, at : at + half, :] = block.reshape(sources, half, V)
                    order = (i // rows == j) & (i % rows == 2 * p + e)
                    more = tail_acc[e, :, p * V : (p + 1) * V].astype(BF16)
                    tail += dot(jnp.where(order, 1.0, 0.0).astype(BF16), more)
            out_ref[:, n * MAIN :, :] = tail.reshape(sources, rows, V).astype(BF16)


def project(got, weight, at, skip, parts, state, final):
    sources = got.shape[0]
    hidden = weight.shape[1]
    half = MAIN // 2
    main_shape, tail_shape = (2, sources * half, hidden), (2, sources, hidden)
    in_specs = [resident(), pl.BlockSpec((2, hidden, V), lambda p: (0, 0, at + p))]
    args = [got, in_hbm(weight)]
    if state is not None:
        in_specs += [resident(), resident()]
        args += list(state)
    scratch = [pltpu.VMEM((sources * (got.shape[1] % MAIN), V), BF16)]
    if final:
        shape = (sources, block_rows(hidden // V), V)
        out_specs, out_shape = resident(), jax.ShapeDtypeStruct(shape, BF16)
        scratch = [pltpu.VMEM(main_shape, F32), pltpu.VMEM(tail_shape, F32)] + scratch
    else:
        out_specs = [resident(), resident()]
        out_shape = [jax.ShapeDtypeStruct(main_shape, F32), jax.ShapeDtypeStruct(tail_shape, F32)]
    return pl.pallas_call(
        functools.partial(project_kernel, skip, parts, state is not None, final),
        grid=(parts,),
        in_specs=in_specs,
        out_specs=out_specs,
        out_shape=out_shape,
        scratch_shapes=scratch,
        compiler_params=params(20),
        cost_estimate=cost(4 * sources * 17 * hidden * V * parts, 2 * got.size + 4 * hidden * V * parts + 16 * sources * 17 * hidden),
        name="project",
    )(*args)


FINISH_STEP = 256


def finish_kernel(code_ref, prob_ref, act_ref, back_ref, grad_act_ref, grad_prob_ref):
    code = code_ref[...]
    column, row = code >> SHIFT, code & MASK
    sources = back_ref.shape[0]
    hidden = act_ref.shape[1]
    n = hidden // V
    steps = code.shape[0]
    main_id = jnp.where(row < MAIN, column * MAIN + row, -1)
    lanes = lax.broadcasted_iota(jnp.int32, (steps, sources * MAIN), 1)
    pick = jnp.where(lanes == main_id, 1.0, 0.0).astype(BF16)
    rows = tail_size(n)
    tail = back_ref[:, n * MAIN :, :].astype(F32).reshape(sources * rows, V).astype(BF16)
    lanes = lax.broadcasted_iota(jnp.int32, (steps, sources * rows), 1)
    prob = prob_ref[...]
    total = jnp.zeros((steps, 1), F32)
    for p in range(n):
        main = back_ref[:, p * MAIN : (p + 1) * MAIN, :].reshape(sources * MAIN, V)
        tail_id = jnp.where(row >= MAIN, column * rows + 2 * p + (row - MAIN), -1)
        proj = dot(pick, main) + dot(jnp.where(lanes == tail_id, 1.0, 0.0).astype(BF16), tail)
        act = act_ref[:, p * V : (p + 1) * V].astype(F32)
        total += jnp.sum(act * proj, axis=1, keepdims=True)
        grad_act_ref[:, p * V : (p + 1) * V] = (prob * proj).astype(BF16)
    grad_prob_ref[...] = total


def finish(code, prob, act, back):
    routes, hidden = act.shape
    one = pl.BlockSpec((FINISH_STEP, 1), lambda i: (i, 0))
    rows = pl.BlockSpec((FINISH_STEP, hidden), lambda i: (i, 0))
    return pl.pallas_call(
        finish_kernel,
        grid=(routes // FINISH_STEP,),
        in_specs=[one, one, rows, resident()],
        out_specs=[rows, one],
        out_shape=[jax.ShapeDtypeStruct((routes, hidden), BF16), jax.ShapeDtypeStruct((routes, 1), F32)],
        compiler_params=params(24),
        cost_estimate=cost(2 * routes * routes * hidden, 2 * (back.size + 2 * routes * hidden)),
        name="finish",
    )(code, prob, act, back)


def place_kernel(column, first, sources_ref, *refs):
    blocks, (out_ref, sems) = refs[:4], refs[-2:]
    copies = []
    for d, block in enumerate(blocks):
        rows, size = block.shape
        row = pl.multiple_of(sources_ref[d] * rows, rows)
        copies.append(
            pltpu.make_async_copy(block, out_ref.at[pl.ds(row, rows), pl.ds(column, size)], sems.at[d])
        )
    for copy in copies:
        copy.start()
    for copy in copies:
        copy.wait()


def place(sources, blocks, own, hidden, width, column):
    first = own is None
    args = [sources, *blocks] + ([] if first else [own])
    anywhere = pl.BlockSpec(memory_space=pl.ANY)
    return pl.pallas_call(
        functools.partial(place_kernel, column, first),
        in_specs=[pl.BlockSpec(memory_space=pltpu.SMEM)] + [anywhere] * (len(args) - 1),
        out_specs=anywhere,
        out_shape=jax.ShapeDtypeStruct((hidden, width), BF16),
        scratch_shapes=[pltpu.SemaphoreType.DMA((len(blocks),))],
        input_output_aliases={} if first else {len(args) - 1: 0},
        compiler_params=params(4),
        cost_estimate=cost(0, 4 * hidden * blocks[0].shape[1]),
        name="place",
    )(*args)


def route_codes(routes, columns):
    tok, top = routes.shape
    experts = 2 * columns
    base = MAIN // 2
    hit = routes[:, :, None] == jnp.arange(experts)[None, None, :]
    member = jnp.any(hit, axis=1).astype(BF16)
    lower = (jnp.arange(tok)[:, None] > jnp.arange(tok)[None, :]).astype(BF16)
    rank = dot(lower, member)
    rank = jnp.sum(jnp.where(hit, rank[:, None, :], 0.0), axis=2).astype(jnp.int32)
    low = routes % 2
    row = jnp.where(rank < base, low * base + rank, MAIN + low)
    return ((routes // 2) << SHIFT) + row


def shards(grad_out, routes, probs, hidden_act, placement, down_weight):
    groups = lax.axis_size("grp")
    columns = lax.axis_size("sp")
    my_group = lax.axis_index("grp")
    my_column = lax.axis_index("sp")
    tok, width = grad_out.shape
    top = routes.shape[1]
    hidden = hidden_act.shape[2]
    quarter = hidden // groups
    act_parts = hidden // V
    last = len(CHUNKS) - 1

    codes = route_codes(routes, columns)
    flat = codes.reshape(1, tok * top)
    prob = probs.astype(F32)
    act = hidden_act.reshape(tok * top, hidden)

    def exchange(v):
        return lax.all_to_all(v, "sp", 0, 0, tiled=True)

    held = lax.dynamic_index_in_dim(placement, my_column, 1, keepdims=False) - 2 * my_column
    hops = [[(i, (i + d) % groups) for i in range(groups)] for d in range(groups)]

    def reduced(part):
        size = part.shape[-1]
        flat_part = part.reshape(groups * 2 * quarter, size)
        return lax.psum_scatter(flat_part, "grp", scatter_dimension=0, tiled=True).reshape(2, quarter, size)

    def wanted(mine):
        out = []
        for d in range(groups):
            which = lax.dynamic_index_in_dim(held, (my_group + d) % groups, 0, keepdims=False)
            out.append(jnp.where(which == 0, mine[0], mine[1]))
        return out

    def moved(sends):
        return [lax.ppermute(sends[d], "grp", hops[d]) if d else sends[d] for d in range(groups)]

    sources = jnp.stack([(my_group + groups - d) % groups for d in range(groups)]).astype(jnp.int32)

    codes_t = codes.T
    first = send_first(codes_t, flat, prob.reshape(1, tok * top), act, grad_out, columns, CHUNKS[0])
    got = {0: exchange(first)}
    outs = send_rest(codes_t, grad_out, columns, CHUNKS[0], CHUNKS[1:])
    got[0], outs = tie(got[0], outs)
    outs = dict(enumerate(outs, 1))

    starts = [sum(CHUNKS[:c]) for c in range(last + 1)]
    mine, sends = {}, {}
    state = None
    acts, part = weight_first(got[0], hidden, CHUNKS[0], groups)
    for c in range(last + 1):
        if c:
            if c == last:
                sends[c - 2] = wanted(mine[c - 2])
                got[c], state, blocks = lax.optimization_barrier((got[c], state, moved(sends[c - 2])))
            part = weight_rest(acts, got[c], CHUNKS[c], groups)
        mine[c] = reduced(part)
        if c < last:
            got[c + 1] = exchange(outs[c + 1])
            skip = act_parts if c == 0 else 0
            state = project(got[c], down_weight, starts[c], skip, CHUNKS[c], state, False)
    proj = project(got[last], down_weight, starts[last], 0, CHUNKS[last], state, True)
    proj, sends[last - 1] = tie(proj, wanted(mine[last - 1]))
    back = exchange(proj)
    grad_act, grad_prob = finish(codes.reshape(tok * top, 1), prob.reshape(tok * top, 1), act, back)
    mine[last], grad_act, grad_prob = lax.optimization_barrier((mine[last], grad_act, grad_prob))
    own = None
    for c in range(last + 1):
        if c not in sends:
            sends[c] = wanted(mine[c])
        own = place(sources, moved(sends[c]) if c else blocks, own, hidden, width, starts[c] * V)
    return (
        grad_act.reshape(tok, top, hidden),
        grad_prob.reshape(tok, top),
        own.reshape(1, 1, hidden, width),
    )


def solution(mesh):
    placed = (
        P(("grp", "sp"), None),
        P(("grp", "sp"), None),
        P(("grp", "sp"), None),
        P(("grp", "sp"), None, None),
        P(),
        P("sp", None, None),
    )
    return jax.shard_map(
        shards,
        mesh=mesh,
        in_specs=placed,
        out_specs=(
            P(("grp", "sp"), None, None),
            P(("grp", "sp"), None),
            P("grp", "sp", None, None),
        ),
        check_vma=False,
    )
```

```python
import functools

import jax
import jax.numpy as jnp
from jax import lax
from jax.experimental import pallas as pl
from jax.experimental.pallas import tpu as pltpu
from jax.sharding import PartitionSpec as P

V = 256
MAIN = 32
LANES = 128
SHIFT = 6
MASK = (1 << SHIFT) - 1
CHUNKS = (4, 6, 6)
DEFER = False
BF16 = jnp.bfloat16
F32 = jnp.float32
MIB = 1024 * 1024


def tie(first, second):
    return lax.optimization_barrier((first, second))


def dot(a, b, dims=((1,), (0,))):
    return lax.dot_general(a, b, (dims, ((), ())), preferred_element_type=F32)


def cost(flops, bytes_accessed):
    return pl.CostEstimate(flops=int(flops), bytes_accessed=int(bytes_accessed), transcendentals=0)


def params(mib):
    return pltpu.CompilerParams(vmem_limit_bytes=mib * MIB)


def resident():
    return pl.BlockSpec(memory_space=pltpu.VMEM)


def in_hbm(x):
    return pltpu.with_memory_space_constraint(x, pltpu.HBM)


def whole(shape):
    return pl.BlockSpec(shape, lambda *_: (0,) * len(shape))


def tail_size(n):
    return (2 * n + 7) // 8 * 8


def block_rows(n):
    return MAIN * n + tail_size(n)


SEND_STEP = 8


def main_ids(first, rows):
    i = lax.broadcasted_iota(jnp.int32, (rows, 1), 0)
    return ((first + i // MAIN) << SHIFT) + i % MAIN


def tail_ids(first, size, part):
    i = lax.broadcasted_iota(jnp.int32, (SEND_STEP * size, 1), 0)
    r = i % size
    return jnp.where(r // 2 == part, ((first + i // size) << SHIFT) + MAIN + r % 2, -1)


def hits(ids, codes):
    found = ids == codes[0:1, :]
    for k in range(1, codes.shape[0]):
        found = found | (ids == codes[k : k + 1, :])
    return jnp.where(found, 1.0, 0.0).astype(BF16)


def store_main(out_ref, part, values):
    out_ref[:, part * MAIN : (part + 1) * MAIN, :] = values.astype(BF16).reshape(SEND_STEP, MAIN, V)


def send_first_kernel(codes_ref, flat_ref, prob_ref, act_ref, grad_ref, out_ref):
    first = pl.program_id(0) * SEND_STEP
    codes, flat, prob = codes_ref[...], flat_ref[...], prob_ref[...]
    ids = main_ids(first, SEND_STEP * MAIN)
    pick = jnp.where(ids == flat, prob, 0.0).astype(BF16)
    act_parts = act_ref.shape[1] // V
    grad = grad_ref[...]
    parts = grad.shape[1] // V
    size = tail_size(act_parts + parts)
    tail = jnp.zeros((SEND_STEP * size, V), F32)
    for p in range(act_parts):
        act = act_ref[:, p * V : (p + 1) * V]
        store_main(out_ref, p, dot(pick, act))
        tail += dot(jnp.where(tail_ids(first, size, p) == flat, prob, 0.0).astype(BF16), act)
    grads = hits(ids, codes)
    for p in range(parts):
        part = grad[:, p * V : (p + 1) * V]
        store_main(out_ref, act_parts + p, dot(grads, part))
        tail += dot(hits(tail_ids(first, size, act_parts + p), codes), part)
    out_ref[:, out_ref.shape[1] - size :, :] = tail.astype(BF16).reshape(SEND_STEP, size, V)


def send_kernel(start, chunks, codes_ref, grad_ref, *out_refs):
    first = pl.program_id(0) * SEND_STEP
    codes = codes_ref[...]
    grads = hits(main_ids(first, SEND_STEP * MAIN), codes)
    at = start * V
    for n, out_ref in zip(chunks, out_refs):
        size = tail_size(n)
        tail = jnp.zeros((SEND_STEP * size, V), F32)
        for p in range(n):
            part = grad_ref[:, at : at + V]
            store_main(out_ref, p, dot(grads, part))
            tail += dot(hits(tail_ids(first, size, p), codes), part)
            at += V
        out_ref[:, MAIN * n :, :] = tail.astype(BF16).reshape(SEND_STEP, size, V)


def send_first(codes, flat, prob, act, grad, columns, parts):
    routes, hidden = act.shape
    tok = grad.shape[0]
    rows = block_rows(hidden // V + parts)
    return pl.pallas_call(
        send_first_kernel,
        grid=(columns // SEND_STEP,),
        in_specs=[
            whole(codes.shape),
            whole(flat.shape),
            whole(prob.shape),
            whole(act.shape),
            pl.BlockSpec((tok, parts * V), lambda i: (0, 0)),
        ],
        out_specs=pl.BlockSpec((SEND_STEP, rows, V), lambda i: (i, 0, 0)),
        out_shape=jax.ShapeDtypeStruct((columns, rows, V), BF16),
        compiler_params=params(24),
        cost_estimate=cost(2 * columns * MAIN * routes * hidden, 2 * columns * rows * V + 2 * routes * hidden),
        name="send_first",
    )(codes, flat, prob, act, grad)


def send_rest(codes, grad, columns, start, chunks):
    tok, width = grad.shape
    shapes = [(columns, block_rows(n), V) for n in chunks]
    return pl.pallas_call(
        functools.partial(send_kernel, start, chunks),
        grid=(columns // SEND_STEP,),
        in_specs=[whole(codes.shape), whole(grad.shape)],
        out_specs=[pl.BlockSpec((SEND_STEP, s[1], V), lambda i: (i, 0, 0)) for s in shapes],
        out_shape=[jax.ShapeDtypeStruct(s, BF16) for s in shapes],
        compiler_params=params(24),
        cost_estimate=cost(2 * columns * MAIN * tok * width, 2 * columns * 34 * width + 2 * tok * width),
        name="send_rest",
    )(codes, grad)


def load_tail(got_ref, tail_ref):
    sources, rows, _ = got_ref.shape
    n = rows // MAIN
    for h in range(V // LANES):
        part = got_ref[:, n * MAIN :, h * LANES : (h + 1) * LANES].astype(F32)
        tail_ref[h] = part.reshape(tail_ref.shape[1:])


def tail_rows(tail_ref, sources, part, expert):
    size = tail_ref.shape[1] // sources
    rows = [tail_ref[h, pl.ds(2 * part + expert, sources, stride=size), :] for h in range(V // LANES)]
    return jnp.concatenate(rows, axis=1).astype(BF16)


def main_rows(got_ref, part, expert):
    half = MAIN // 2
    rows = got_ref[:, pl.ds(part * MAIN + expert * half, half), :]
    return rows.reshape(got_ref.shape[0] * half, V)


def weight_step(acts, rows, more, keep_ref, send_ref, expert):
    depth = rows.shape[0]
    total = dot(acts[:, :depth], rows) + dot(acts[:, depth:], more)
    half = total.shape[0] // 2
    keep_ref[expert] = total[:half].astype(BF16)
    send_ref[...] = total[half:].astype(BF16)


def weight_first_kernel(act_parts, order_ref, got_ref, acts_ref, keep_ref, low_ref, high_ref, tail_ref, plain_ref):
    sources = got_ref.shape[0]
    part = pl.program_id(0)

    @pl.when(part == 0)
    def _():
        load_tail(got_ref, tail_ref)
        quarters = order_ref.shape[1]
        size = acts_ref.shape[1] // quarters
        for e in range(2):
            for p in range(act_parts):
                block = main_rows(got_ref, p, e)
                more = tail_rows(tail_ref, sources, p, e)
                plain_ref[p * V : (p + 1) * V, : block.shape[0]] = block.astype(F32).T.astype(BF16)
                plain_ref[p * V : (p + 1) * V, block.shape[0] :] = more.astype(F32).T.astype(BF16)
            for q in range(quarters):
                at = pl.multiple_of(order_ref[e, q] * size, size)
                acts_ref[e, q * size : (q + 1) * size, :] = plain_ref[pl.ds(at, size), :]

    for e, send_ref in enumerate((low_ref, high_ref)):
        more = tail_rows(tail_ref, sources, act_parts + part, e)
        weight_step(acts_ref[e], main_rows(got_ref, act_parts + part, e), more, keep_ref, send_ref, e)


def weight_kernel(acts_ref, got_ref, keep_ref, low_ref, high_ref, tail_ref):
    sources = got_ref.shape[0]
    part = pl.program_id(0)

    @pl.when(part == 0)
    def _():
        load_tail(got_ref, tail_ref)

    for e, send_ref in enumerate((low_ref, high_ref)):
        more = tail_rows(tail_ref, sources, part, e)
        weight_step(acts_ref[e], main_rows(got_ref, part, e), more, keep_ref, send_ref, e)


def sum_specs(hidden, parts):
    half = hidden // 2
    specs = [pl.BlockSpec((2, half, V), lambda p: (0, 0, p))] + [pl.BlockSpec((half, V), lambda p: (0, p))] * 2
    shapes = [pltpu.HBM((2, half, parts * V), BF16)] + [pltpu.HBM((half, parts * V), BF16)] * 2
    return specs, shapes


def tail_scratch(got):
    return pltpu.VMEM((V // LANES, got.shape[0] * (got.shape[1] % MAIN), LANES), F32)


def weight_first(order, got, hidden, parts):
    depth = got.shape[0] * (MAIN // 2 + 1)
    specs, shapes = sum_specs(hidden, parts)
    return pl.pallas_call(
        functools.partial(weight_first_kernel, hidden // V),
        grid=(parts,),
        in_specs=[pl.BlockSpec(memory_space=pltpu.SMEM), resident()],
        out_specs=[whole((2, hidden, depth))] + specs,
        out_shape=[pltpu.HBM((2, hidden, depth), BF16)] + shapes,
        scratch_shapes=[tail_scratch(got), pltpu.VMEM((hidden, depth), BF16)],
        compiler_params=params(16),
        cost_estimate=cost(4 * depth * hidden * V * parts, 2 * (got.size + 4 * depth * hidden)),
        name="weight_first",
    )(order, got)


def weight_rest(acts, got, parts):
    hidden, depth = acts.shape[1:]
    specs, shapes = sum_specs(hidden, parts)
    return pl.pallas_call(
        weight_kernel,
        grid=(parts,),
        in_specs=[whole(acts.shape), resident()],
        out_specs=specs,
        out_shape=shapes,
        scratch_shapes=[tail_scratch(got)],
        compiler_params=params(16),
        cost_estimate=cost(4 * depth * hidden * V * parts, 2 * (got.size + acts.size + 2 * hidden * V * parts)),
        name="weight_rest",
    )(in_hbm(acts), got)


def project_kernel(skip, parts, chained, final, *refs):
    refs = list(refs)
    got_ref, weight_ref = refs[:2]
    refs = refs[2:]
    if chained:
        main_in, tail_in = refs[:2]
        refs = refs[2:]
    if final:
        out_ref, main_acc, tail_acc, tail_ref = refs
    else:
        main_acc, tail_acc, tail_ref = refs
    sources = got_ref.shape[0]
    half = MAIN // 2
    part = pl.program_id(0)

    @pl.when(part == 0)
    def _():
        load_tail(got_ref, tail_ref)
        if chained:
            main_acc[...] = main_in[...]
            tail_acc[...] = tail_in[...]
        else:
            main_acc[...] = jnp.zeros_like(main_acc)
            tail_acc[...] = jnp.zeros_like(tail_acc)

    for e in range(2):
        weight = weight_ref[e]
        rows = main_rows(got_ref, part + skip, e)
        main_acc[e] += dot(rows, weight, ((1,), (1,)))
        more = tail_rows(tail_ref, sources, part + skip, e)
        tail_acc[e] += dot(more, weight, ((1,), (1,)))

    if final:

        @pl.when(part == parts - 1)
        def _():
            hidden = weight_ref.shape[1]
            n = hidden // V
            rows = tail_size(n)
            size = sources * rows
            i = lax.broadcasted_iota(jnp.int32, (size, sources), 0)
            j = lax.broadcasted_iota(jnp.int32, (size, sources), 1)
            tail = jnp.zeros((size, V), F32)
            for e in range(2):
                for p in range(n):
                    block = main_acc[e, :, p * V : (p + 1) * V].astype(BF16)
                    at = p * MAIN + e * half
                    out_ref[:, at : at + half, :] = block.reshape(sources, half, V)
                    order = (i // rows == j) & (i % rows == 2 * p + e)
                    more = tail_acc[e, :, p * V : (p + 1) * V].astype(BF16)
                    tail += dot(jnp.where(order, 1.0, 0.0).astype(BF16), more)
            out_ref[:, n * MAIN :, :] = tail.reshape(sources, rows, V).astype(BF16)


def project(got, weight, at, skip, parts, state, final):
    sources = got.shape[0]
    hidden = weight.shape[1]
    half = MAIN // 2
    main_shape, tail_shape = (2, sources * half, hidden), (2, sources, hidden)
    in_specs = [resident(), pl.BlockSpec((2, hidden, V), lambda p: (0, 0, at + p))]
    args = [got, in_hbm(weight)]
    if state is not None:
        in_specs += [resident(), resident()]
        args += list(state)
    scratch = [pltpu.VMEM((V // LANES, sources * (got.shape[1] % MAIN), LANES), F32)]
    if final:
        shape = (sources, block_rows(hidden // V), V)
        out_specs, out_shape = resident(), jax.ShapeDtypeStruct(shape, BF16)
        scratch = [pltpu.VMEM(main_shape, F32), pltpu.VMEM(tail_shape, F32)] + scratch
    else:
        out_specs = [resident(), resident()]
        out_shape = [jax.ShapeDtypeStruct(main_shape, F32), jax.ShapeDtypeStruct(tail_shape, F32)]
    return pl.pallas_call(
        functools.partial(project_kernel, skip, parts, state is not None, final),
        grid=(parts,),
        in_specs=in_specs,
        out_specs=out_specs,
        out_shape=out_shape,
        scratch_shapes=scratch,
        compiler_params=params(20),
        cost_estimate=cost(4 * sources * 17 * hidden * V * parts, 2 * got.size + 4 * hidden * V * parts + 16 * sources * 17 * hidden),
        name="project",
    )(*args)


FINISH_STEP = 256


def finish_kernel(code_ref, prob_ref, act_ref, back_ref, grad_act_ref, grad_prob_ref):
    code = code_ref[...]
    column, row = code >> SHIFT, code & MASK
    sources = back_ref.shape[0]
    hidden = act_ref.shape[1]
    n = hidden // V
    steps = code.shape[0]
    main_id = jnp.where(row < MAIN, column * MAIN + row, -1)
    lanes = lax.broadcasted_iota(jnp.int32, (steps, sources * MAIN), 1)
    pick = jnp.where(lanes == main_id, 1.0, 0.0).astype(BF16)
    rows = tail_size(n)
    tail = back_ref[:, n * MAIN :, :].astype(F32).reshape(sources * rows, V).astype(BF16)
    lanes = lax.broadcasted_iota(jnp.int32, (steps, sources * rows), 1)
    prob = prob_ref[...]
    total = jnp.zeros((steps, 1), F32)
    for p in range(n):
        main = back_ref[:, p * MAIN : (p + 1) * MAIN, :].reshape(sources * MAIN, V)
        tail_id = jnp.where(row >= MAIN, column * rows + 2 * p + (row - MAIN), -1)
        proj = dot(pick, main) + dot(jnp.where(lanes == tail_id, 1.0, 0.0).astype(BF16), tail)
        act = act_ref[:, p * V : (p + 1) * V].astype(F32)
        total += jnp.sum(act * proj, axis=1, keepdims=True)
        grad_act_ref[:, p * V : (p + 1) * V] = (prob * proj).astype(BF16)
    grad_prob_ref[...] = total


def finish(code, prob, act, back):
    routes, hidden = act.shape
    one = pl.BlockSpec((FINISH_STEP, 1), lambda i: (i, 0))
    rows = pl.BlockSpec((FINISH_STEP, hidden), lambda i: (i, 0))
    return pl.pallas_call(
        finish_kernel,
        grid=(routes // FINISH_STEP,),
        in_specs=[one, one, rows, resident()],
        out_specs=[rows, one],
        out_shape=[jax.ShapeDtypeStruct((routes, hidden), BF16), jax.ShapeDtypeStruct((routes, 1), F32)],
        compiler_params=params(24),
        cost_estimate=cost(2 * routes * routes * hidden, 2 * (back.size + 2 * routes * hidden)),
        name="finish",
    )(code, prob, act, back)


def place_kernel(column, sources_ref, *refs):
    blocks, (out_ref, sems) = refs[:4], refs[-2:]
    copies = []
    for d, block in enumerate(blocks):
        rows, size = block.shape
        row = pl.multiple_of(sources_ref[d] * rows, rows)
        copies.append(
            pltpu.make_async_copy(block, out_ref.at[pl.ds(row, rows), pl.ds(column, size)], sems.at[d])
        )
    for copy in copies:
        copy.start()
    for copy in copies:
        copy.wait()


def place(sources, blocks, own, hidden, width, column):
    first = own is None
    args = [sources, *blocks] + ([] if first else [own])
    own_spec = pl.BlockSpec(memory_space=pltpu.HBM)
    return pl.pallas_call(
        functools.partial(place_kernel, column),
        in_specs=[pl.BlockSpec(memory_space=pltpu.SMEM)] + [resident()] * len(blocks) + [own_spec] * (not first),
        out_specs=own_spec,
        out_shape=pltpu.HBM((hidden, width), BF16),
        scratch_shapes=[pltpu.SemaphoreType.DMA((len(blocks),))],
        input_output_aliases={} if first else {len(args) - 1: 0},
        compiler_params=params(4),
        cost_estimate=cost(0, 4 * hidden * blocks[0].shape[1]),
        name="place",
    )(*args)


def route_codes(routes, columns):
    tok, top = routes.shape
    experts = 2 * columns
    base = MAIN // 2
    hit = routes[:, :, None] == jnp.arange(experts)[None, None, :]
    member = jnp.any(hit, axis=1).astype(BF16)
    lower = (jnp.arange(tok)[:, None] > jnp.arange(tok)[None, :]).astype(BF16)
    rank = dot(lower, member)
    rank = jnp.sum(jnp.where(hit, rank[:, None, :], 0.0), axis=2).astype(jnp.int32)
    low = routes % 2
    row = jnp.where(rank < base, low * base + rank, MAIN + low)
    return ((routes // 2) << SHIFT) + row


def shards(grad_out, routes, probs, hidden_act, placement, down_weight):
    groups = lax.axis_size("grp")
    columns = lax.axis_size("sp")
    my_group = lax.axis_index("grp")
    my_column = lax.axis_index("sp")
    tok, width = grad_out.shape
    top = routes.shape[1]
    hidden = hidden_act.shape[2]
    quarter = hidden // groups
    act_parts = hidden // V
    last = len(CHUNKS) - 1

    codes = route_codes(routes, columns)
    flat = codes.reshape(1, tok * top)
    prob = probs.astype(F32)
    act = hidden_act.reshape(tok * top, hidden)

    def exchange(v):
        return lax.all_to_all(v, "sp", 0, 0, tiled=True)

    held = lax.dynamic_index_in_dim(placement, my_column, 1, keepdims=False) - 2 * my_column
    hops = [[(i, (i + d) % groups) for i in range(groups)] for d in range(groups)]

    near = [(0, 1), (1, 0), (2, 3), (3, 2)]
    far = [(0, 3), (3, 0), (1, 2), (2, 1)]
    g = my_group.astype(jnp.int32)
    order = jnp.stack(
        [jnp.stack([g, 3 - g, g ^ 1, 3 - (g ^ 1)]), jnp.stack([g, g ^ 1, 3 - g, 3 - (g ^ 1)])]
    )

    def first_round(low, high):
        return lax.ppermute(low, "grp", near), lax.ppermute(high, "grp", far)

    def forwarded(keep, came):
        return [(keep[e, quarter:].astype(F32) + came[e][quarter:].astype(F32)).astype(BF16) for e in range(2)]

    def second_round(low, high):
        return lax.ppermute(low, "grp", far), lax.ppermute(high, "grp", near)

    def completed(keep, came, last_came):
        return [
            (keep[e, :quarter].astype(F32) + came[e][:quarter].astype(F32) + last_came[e].astype(F32)).astype(BF16)
            for e in range(2)
        ]

    def wanted(mine):
        out = []
        for d in range(groups):
            which = lax.dynamic_index_in_dim(held, (my_group + d) % groups, 0, keepdims=False)
            out.append(jnp.where(which == 0, mine[0], mine[1]))
        return out

    def moved(sends):
        return [lax.ppermute(sends[d], "grp", hops[d]) if d else sends[d] for d in range(groups)]

    sources = jnp.stack([(my_group + groups - d) % groups for d in range(groups)]).astype(jnp.int32)

    codes_t = codes.T
    first = send_first(codes_t, flat, prob.reshape(1, tok * top), act, grad_out, columns, CHUNKS[0])
    got = {0: exchange(first)}
    outs = send_rest(codes_t, grad_out, columns, CHUNKS[0], CHUNKS[1:])
    got[0], outs = tie(got[0], outs)
    outs = dict(enumerate(outs, 1))

    starts = [sum(CHUNKS[:c]) for c in range(last + 1)]
    sends, blocks = {}, {}
    state = None
    barrier = lax.optimization_barrier
    for c in range(last + 1):
        if c == 0:
            acts, keep, low, high = weight_first(order, got[0], hidden, CHUNKS[0])
        else:
            got[c], sends[c - 1] = barrier((got[c], sends[c - 1]))
            if c == last:
                got[c], state = barrier((got[c], state))
            keep, low, high = weight_rest(acts, got[c], CHUNKS[c])
        if c < last:
            outs[c + 1], low, high = barrier((outs[c + 1], low, high))
            got[c + 1] = exchange(outs[c + 1])
            skip = act_parts if c == 0 else 0
            state = project(got[c], down_weight, starts[c], skip, CHUNKS[c], state, False)
        came = first_round(low, high)
        if c == last:
            proj = project(got[last], down_weight, starts[last], 0, CHUNKS[last], state, True)
            back = exchange(proj)
            grad_act, grad_prob = finish(codes.reshape(tok * top, 1), prob.reshape(tok * top, 1), act, back)
        if c >= 2:
            came, blocks[c - 2] = barrier((came, blocks[c - 2]))
        passed = forwarded(keep, came)
        if c >= 1:
            if DEFER:
                passed, sends[c - 1] = barrier((passed, sends[c - 1]))
            blocks[c - 1] = moved(sends[c - 1])
        last_came = second_round(*passed)
        if c == last:
            last_came, grad_act, grad_prob = barrier((last_came, grad_act, grad_prob))
        sends[c] = wanted(completed(keep, came, last_came))
    blocks[last] = moved(sends[last])
    own = None
    for c in range(last + 1):
        own = place(sources, blocks[c], own, hidden, width, starts[c] * V)
    return (
        grad_act.reshape(tok, top, hidden),
        grad_prob.reshape(tok, top),
        own.reshape(1, 1, hidden, width),
    )


def solution(mesh):
    placed = (
        P(("grp", "sp"), None),
        P(("grp", "sp"), None),
        P(("grp", "sp"), None),
        P(("grp", "sp"), None, None),
        P(),
        P("sp", None, None),
    )
    return jax.shard_map(
        shards,
        mesh=mesh,
        in_specs=placed,
        out_specs=(
            P(("grp", "sp"), None, None),
            P(("grp", "sp"), None),
            P("grp", "sp", None, None),
        ),
        check_vma=False,
    )
```

```python
import functools

import jax
import jax.numpy as jnp
from jax import lax
from jax.experimental import pallas as pl
from jax.experimental.pallas import tpu as pltpu
from jax.sharding import PartitionSpec as P

V = 256
MAIN = 32
LANES = 128
SHIFT = 6
MASK = (1 << SHIFT) - 1
CHUNKS = (4, 6, 6)
BF16 = jnp.bfloat16
F32 = jnp.float32
MIB = 1024 * 1024


def tie(first, second):
    return lax.optimization_barrier((first, second))


def dot(a, b, dims=((1,), (0,))):
    return lax.dot_general(a, b, (dims, ((), ())), preferred_element_type=F32)


def cost(flops, bytes_accessed):
    return pl.CostEstimate(flops=int(flops), bytes_accessed=int(bytes_accessed), transcendentals=0)


def params(mib):
    return pltpu.CompilerParams(vmem_limit_bytes=mib * MIB)


def resident():
    return pl.BlockSpec(memory_space=pltpu.VMEM)


def in_hbm(x):
    return pltpu.with_memory_space_constraint(x, pltpu.HBM)


def whole(shape):
    return pl.BlockSpec(shape, lambda *_: (0,) * len(shape))


def tail_size(n):
    return (2 * n + 7) // 8 * 8


def block_rows(n):
    return MAIN * n + tail_size(n)


SEND_STEP = 8


def main_ids(first, rows):
    i = lax.broadcasted_iota(jnp.int32, (rows, 1), 0)
    return ((first + i // MAIN) << SHIFT) + i % MAIN


def tail_ids(first, size, part):
    i = lax.broadcasted_iota(jnp.int32, (SEND_STEP * size, 1), 0)
    r = i % size
    return jnp.where(r // 2 == part, ((first + i // size) << SHIFT) + MAIN + r % 2, -1)


def hits(ids, codes):
    found = ids == codes[0:1, :]
    for k in range(1, codes.shape[0]):
        found = found | (ids == codes[k : k + 1, :])
    return jnp.where(found, 1.0, 0.0).astype(BF16)


def store_main(out_ref, part, values):
    out_ref[:, part * MAIN : (part + 1) * MAIN, :] = values.astype(BF16).reshape(SEND_STEP, MAIN, V)


def send_first_kernel(codes_ref, flat_ref, prob_ref, act_ref, grad_ref, out_ref):
    first = pl.program_id(0) * SEND_STEP
    codes, flat, prob = codes_ref[...], flat_ref[...], prob_ref[...]
    ids = main_ids(first, SEND_STEP * MAIN)
    pick = jnp.where(ids == flat, prob, 0.0).astype(BF16)
    act_parts = act_ref.shape[1] // V
    grad = grad_ref[...]
    parts = grad.shape[1] // V
    size = tail_size(act_parts + parts)
    tail = jnp.zeros((SEND_STEP * size, V), F32)
    for p in range(act_parts):
        act = act_ref[:, p * V : (p + 1) * V]
        store_main(out_ref, p, dot(pick, act))
        tail += dot(jnp.where(tail_ids(first, size, p) == flat, prob, 0.0).astype(BF16), act)
    grads = hits(ids, codes)
    for p in range(parts):
        part = grad[:, p * V : (p + 1) * V]
        store_main(out_ref, act_parts + p, dot(grads, part))
        tail += dot(hits(tail_ids(first, size, act_parts + p), codes), part)
    out_ref[:, out_ref.shape[1] - size :, :] = tail.astype(BF16).reshape(SEND_STEP, size, V)


def send_kernel(start, chunks, codes_ref, grad_ref, *out_refs):
    first = pl.program_id(0) * SEND_STEP
    codes = codes_ref[...]
    grads = hits(main_ids(first, SEND_STEP * MAIN), codes)
    at = start * V
    for n, out_ref in zip(chunks, out_refs):
        size = tail_size(n)
        tail = jnp.zeros((SEND_STEP * size, V), F32)
        for p in range(n):
            part = grad_ref[:, at : at + V]
            store_main(out_ref, p, dot(grads, part))
            tail += dot(hits(tail_ids(first, size, p), codes), part)
            at += V
        out_ref[:, MAIN * n :, :] = tail.astype(BF16).reshape(SEND_STEP, size, V)


def send_first(codes, flat, prob, act, grad, columns, parts):
    routes, hidden = act.shape
    tok = grad.shape[0]
    rows = block_rows(hidden // V + parts)
    return pl.pallas_call(
        send_first_kernel,
        grid=(columns // SEND_STEP,),
        in_specs=[
            whole(codes.shape),
            whole(flat.shape),
            whole(prob.shape),
            whole(act.shape),
            pl.BlockSpec((tok, parts * V), lambda i: (0, 0)),
        ],
        out_specs=pl.BlockSpec((SEND_STEP, rows, V), lambda i: (i, 0, 0)),
        out_shape=pltpu.HBM((columns, rows, V), BF16),
        compiler_params=params(24),
        cost_estimate=cost(2 * columns * MAIN * routes * hidden, 2 * columns * rows * V + 2 * routes * hidden),
        name="send_first",
    )(codes, flat, prob, in_hbm(act), in_hbm(grad))


def send_rest(codes, grad, columns, start, chunks):
    tok, width = grad.shape
    shapes = [(columns, block_rows(n), V) for n in chunks]
    return pl.pallas_call(
        functools.partial(send_kernel, start, chunks),
        grid=(columns // SEND_STEP,),
        in_specs=[whole(codes.shape), whole(grad.shape)],
        out_specs=[pl.BlockSpec((SEND_STEP, s[1], V), lambda i: (i, 0, 0)) for s in shapes],
        out_shape=[pltpu.HBM(s, BF16) for s in shapes],
        compiler_params=params(24),
        cost_estimate=cost(2 * columns * MAIN * tok * width, 2 * columns * 34 * width + 2 * tok * width),
        name="send_rest",
    )(codes, in_hbm(grad))


def load_tail(got_ref, tail_ref):
    sources, rows, _ = got_ref.shape
    n = rows // MAIN
    for h in range(V // LANES):
        part = got_ref[:, n * MAIN :, h * LANES : (h + 1) * LANES].astype(F32)
        tail_ref[h] = part.reshape(tail_ref.shape[1:])


def tail_rows(tail_ref, sources, part, expert):
    size = tail_ref.shape[1] // sources
    rows = [tail_ref[h, pl.ds(2 * part + expert, sources, stride=size), :] for h in range(V // LANES)]
    return jnp.concatenate(rows, axis=1).astype(BF16)


def main_rows(got_ref, part, expert):
    half = MAIN // 2
    rows = got_ref[:, pl.ds(part * MAIN + expert * half, half), :]
    return rows.reshape(got_ref.shape[0] * half, V)


def parts_a_step(parts):
    return 2 if parts % 2 == 0 else 1


def weight_step(acts, got_ref, tail_ref, part, count, keep_ref, send_ref, expert):
    sources = got_ref.shape[0]
    rows = jnp.concatenate([main_rows(got_ref, part + i, expert) for i in range(count)], axis=1)
    more = jnp.concatenate([tail_rows(tail_ref, sources, part + i, expert) for i in range(count)], axis=1)
    depth = rows.shape[0]
    total = dot(acts[:, :depth], rows) + dot(acts[:, depth:], more)
    half = total.shape[0] // 2
    size = count * V
    at = pl.multiple_of(pl.program_id(0) * size, size)
    keep_ref[expert, :, pl.ds(at, size)] = total[:half].astype(BF16)
    send_ref[:, pl.ds(at, size)] = total[half:].astype(BF16)


def weight_first_kernel(act_parts, order_ref, got_ref, acts_ref, keep_ref, low_ref, high_ref, tail_ref, plain_ref):
    sources = got_ref.shape[0]
    part = pl.program_id(0)

    @pl.when(part == 0)
    def _():
        load_tail(got_ref, tail_ref)
        quarters = order_ref.shape[1]
        size = acts_ref.shape[1] // quarters
        for e in range(2):
            for p in range(act_parts):
                block = main_rows(got_ref, p, e)
                more = tail_rows(tail_ref, sources, p, e)
                plain_ref[p * V : (p + 1) * V, : block.shape[0]] = block.astype(F32).T.astype(BF16)
                plain_ref[p * V : (p + 1) * V, block.shape[0] :] = more.astype(F32).T.astype(BF16)
            for q in range(quarters):
                at = pl.multiple_of(order_ref[e, q] * size, size)
                acts_ref[e, q * size : (q + 1) * size, :] = plain_ref[pl.ds(at, size), :]

    count = parts_a_step(low_ref.shape[1] // V)
    for e, send_ref in enumerate((low_ref, high_ref)):
        weight_step(acts_ref[e], got_ref, tail_ref, act_parts + part * count, count, keep_ref, send_ref, e)


def weight_kernel(acts_ref, got_ref, keep_ref, low_ref, high_ref, tail_ref):
    part = pl.program_id(0)

    @pl.when(part == 0)
    def _():
        load_tail(got_ref, tail_ref)

    count = parts_a_step(low_ref.shape[1] // V)
    for e, send_ref in enumerate((low_ref, high_ref)):
        weight_step(acts_ref[e], got_ref, tail_ref, part * count, count, keep_ref, send_ref, e)


def sum_specs(hidden, parts):
    half = hidden // 2
    specs = [resident()] * 3
    shapes = [jax.ShapeDtypeStruct(s, BF16) for s in ((2, half, parts * V), (half, parts * V), (half, parts * V))]
    return specs, shapes


def tail_scratch(got):
    return pltpu.VMEM((V // LANES, got.shape[0] * (got.shape[1] % MAIN), LANES), F32)


def weight_first(order, got, hidden, parts):
    depth = got.shape[0] * (MAIN // 2 + 1)
    specs, shapes = sum_specs(hidden, parts)
    return pl.pallas_call(
        functools.partial(weight_first_kernel, hidden // V),
        grid=(parts // parts_a_step(parts),),
        in_specs=[pl.BlockSpec(memory_space=pltpu.SMEM), resident()],
        out_specs=[whole((2, hidden, depth))] + specs,
        out_shape=[pltpu.HBM((2, hidden, depth), BF16)] + shapes,
        scratch_shapes=[tail_scratch(got), pltpu.VMEM((hidden, depth), BF16)],
        compiler_params=params(16),
        cost_estimate=cost(4 * depth * hidden * V * parts, 2 * (got.size + 4 * depth * hidden)),
        name="weight_first",
    )(order, got)


def weight_rest(acts, got, parts):
    hidden, depth = acts.shape[1:]
    specs, shapes = sum_specs(hidden, parts)
    return pl.pallas_call(
        weight_kernel,
        grid=(parts // parts_a_step(parts),),
        in_specs=[whole(acts.shape), resident()],
        out_specs=specs,
        out_shape=shapes,
        scratch_shapes=[tail_scratch(got)],
        compiler_params=params(16),
        cost_estimate=cost(4 * depth * hidden * V * parts, 2 * (got.size + acts.size + 2 * hidden * V * parts)),
        name="weight_rest",
    )(in_hbm(acts), got)


def project_kernel(skip, parts, chained, final, *refs):
    refs = list(refs)
    got_ref, weight_ref = refs[:2]
    refs = refs[2:]
    if chained:
        main_in, tail_in = refs[:2]
        refs = refs[2:]
    if final:
        out_ref, main_acc, tail_acc, tail_ref = refs
    else:
        main_acc, tail_acc, tail_ref = refs
    sources = got_ref.shape[0]
    half = MAIN // 2
    part = pl.program_id(0)

    @pl.when(part == 0)
    def _():
        load_tail(got_ref, tail_ref)
        if chained:
            main_acc[...] = main_in[...]
            tail_acc[...] = tail_in[...]
        else:
            main_acc[...] = jnp.zeros_like(main_acc)
            tail_acc[...] = jnp.zeros_like(tail_acc)

    for e in range(2):
        weight = weight_ref[e]
        rows = main_rows(got_ref, part + skip, e)
        main_acc[e] += dot(rows, weight, ((1,), (1,)))
        more = tail_rows(tail_ref, sources, part + skip, e)
        tail_acc[e] += dot(more, weight, ((1,), (1,)))

    if final:

        @pl.when(part == parts - 1)
        def _():
            hidden = weight_ref.shape[1]
            n = hidden // V
            rows = tail_size(n)
            size = sources * rows
            i = lax.broadcasted_iota(jnp.int32, (size, sources), 0)
            j = lax.broadcasted_iota(jnp.int32, (size, sources), 1)
            tail = jnp.zeros((size, V), F32)
            for e in range(2):
                for p in range(n):
                    block = main_acc[e, :, p * V : (p + 1) * V].astype(BF16)
                    at = p * MAIN + e * half
                    out_ref[:, at : at + half, :] = block.reshape(sources, half, V)
                    order = (i // rows == j) & (i % rows == 2 * p + e)
                    more = tail_acc[e, :, p * V : (p + 1) * V].astype(BF16)
                    tail += dot(jnp.where(order, 1.0, 0.0).astype(BF16), more)
            out_ref[:, n * MAIN :, :] = tail.reshape(sources, rows, V).astype(BF16)


def project(got, weight, at, skip, parts, state, final):
    sources = got.shape[0]
    hidden = weight.shape[1]
    half = MAIN // 2
    main_shape, tail_shape = (2, sources * half, hidden), (2, sources, hidden)
    in_specs = [resident(), pl.BlockSpec((2, hidden, V), lambda p: (0, 0, at + p))]
    args = [got, in_hbm(weight)]
    if state is not None:
        in_specs += [resident(), resident()]
        args += list(state)
    scratch = [pltpu.VMEM((V // LANES, sources * (got.shape[1] % MAIN), LANES), F32)]
    if final:
        shape = (sources, block_rows(hidden // V), V)
        out_specs, out_shape = resident(), jax.ShapeDtypeStruct(shape, BF16)
        scratch = [pltpu.VMEM(main_shape, F32), pltpu.VMEM(tail_shape, F32)] + scratch
    else:
        out_specs = [resident(), resident()]
        out_shape = [jax.ShapeDtypeStruct(main_shape, F32), jax.ShapeDtypeStruct(tail_shape, F32)]
    return pl.pallas_call(
        functools.partial(project_kernel, skip, parts, state is not None, final),
        grid=(parts,),
        in_specs=in_specs,
        out_specs=out_specs,
        out_shape=out_shape,
        scratch_shapes=scratch,
        compiler_params=params(20),
        cost_estimate=cost(4 * sources * 17 * hidden * V * parts, 2 * got.size + 4 * hidden * V * parts + 16 * sources * 17 * hidden),
        name="project",
    )(*args)


FINISH_STEP = 256


def finish_kernel(code_ref, prob_ref, act_ref, back_ref, grad_act_ref, grad_prob_ref):
    code = code_ref[...]
    column, row = code >> SHIFT, code & MASK
    sources = back_ref.shape[0]
    hidden = act_ref.shape[1]
    n = hidden // V
    steps = code.shape[0]
    main_id = jnp.where(row < MAIN, column * MAIN + row, -1)
    lanes = lax.broadcasted_iota(jnp.int32, (steps, sources * MAIN), 1)
    pick = jnp.where(lanes == main_id, 1.0, 0.0).astype(BF16)
    rows = tail_size(n)
    tail = back_ref[:, n * MAIN :, :].astype(F32).reshape(sources * rows, V).astype(BF16)
    lanes = lax.broadcasted_iota(jnp.int32, (steps, sources * rows), 1)
    prob = prob_ref[...]
    total = jnp.zeros((steps, 1), F32)
    for p in range(n):
        main = back_ref[:, p * MAIN : (p + 1) * MAIN, :].reshape(sources * MAIN, V)
        tail_id = jnp.where(row >= MAIN, column * rows + 2 * p + (row - MAIN), -1)
        proj = dot(pick, main) + dot(jnp.where(lanes == tail_id, 1.0, 0.0).astype(BF16), tail)
        act = act_ref[:, p * V : (p + 1) * V].astype(F32)
        total += jnp.sum(act * proj, axis=1, keepdims=True)
        grad_act_ref[:, p * V : (p + 1) * V] = (prob * proj).astype(BF16)
    grad_prob_ref[...] = total


def finish(code, prob, act, back):
    routes, hidden = act.shape
    one = pl.BlockSpec((FINISH_STEP, 1), lambda i: (i, 0))
    rows = pl.BlockSpec((FINISH_STEP, hidden), lambda i: (i, 0))
    return pl.pallas_call(
        finish_kernel,
        grid=(routes // FINISH_STEP,),
        in_specs=[one, one, rows, resident()],
        out_specs=[rows, one],
        out_shape=[jax.ShapeDtypeStruct((routes, hidden), BF16), jax.ShapeDtypeStruct((routes, 1), F32)],
        compiler_params=params(24),
        cost_estimate=cost(2 * routes * routes * hidden, 2 * (back.size + 2 * routes * hidden)),
        name="finish",
    )(code, prob, act, back)


def place_kernel(column, sources_ref, *refs):
    blocks, (out_ref, sems) = refs[:4], refs[-2:]
    copies = []
    for d, block in enumerate(blocks):
        rows, size = block.shape
        row = pl.multiple_of(sources_ref[d] * rows, rows)
        copies.append(
            pltpu.make_async_copy(block, out_ref.at[pl.ds(row, rows), pl.ds(column, size)], sems.at[d])
        )
    for copy in copies:
        copy.start()
    for copy in copies:
        copy.wait()


def place(sources, blocks, own, hidden, width, column):
    first = own is None
    args = [sources, *blocks] + ([] if first else [own])
    own_spec = pl.BlockSpec(memory_space=pltpu.HBM)
    return pl.pallas_call(
        functools.partial(place_kernel, column),
        in_specs=[pl.BlockSpec(memory_space=pltpu.SMEM)] + [resident()] * len(blocks) + [own_spec] * (not first),
        out_specs=own_spec,
        out_shape=pltpu.HBM((hidden, width), BF16),
        scratch_shapes=[pltpu.SemaphoreType.DMA((len(blocks),))],
        input_output_aliases={} if first else {len(args) - 1: 0},
        compiler_params=params(4),
        cost_estimate=cost(0, 4 * hidden * blocks[0].shape[1]),
        name="place",
    )(*args)


def route_codes(routes, columns):
    tok, top = routes.shape
    experts = 2 * columns
    base = MAIN // 2
    hit = routes[:, :, None] == jnp.arange(experts)[None, None, :]
    member = jnp.any(hit, axis=1).astype(BF16)
    lower = (jnp.arange(tok)[:, None] > jnp.arange(tok)[None, :]).astype(BF16)
    rank = dot(lower, member)
    rank = jnp.sum(jnp.where(hit, rank[:, None, :], 0.0), axis=2).astype(jnp.int32)
    low = routes % 2
    row = jnp.where(rank < base, low * base + rank, MAIN + low)
    return ((routes // 2) << SHIFT) + row


def shards(grad_out, routes, probs, hidden_act, placement, down_weight):
    groups = lax.axis_size("grp")
    columns = lax.axis_size("sp")
    my_group = lax.axis_index("grp")
    my_column = lax.axis_index("sp")
    tok, width = grad_out.shape
    top = routes.shape[1]
    hidden = hidden_act.shape[2]
    quarter = hidden // groups
    act_parts = hidden // V
    last = len(CHUNKS) - 1

    codes = route_codes(routes, columns)
    flat = codes.reshape(1, tok * top)
    prob = probs.astype(F32)
    act = hidden_act.reshape(tok * top, hidden)

    def exchange(v):
        return lax.all_to_all(v, "sp", 0, 0, tiled=True)

    held = lax.dynamic_index_in_dim(placement, my_column, 1, keepdims=False) - 2 * my_column
    hops = [[(i, (i + d) % groups) for i in range(groups)] for d in range(groups)]

    near = [(0, 1), (1, 0), (2, 3), (3, 2)]
    far = [(0, 3), (3, 0), (1, 2), (2, 1)]
    g = my_group.astype(jnp.int32)
    order = jnp.stack(
        [jnp.stack([g, 3 - g, g ^ 1, 3 - (g ^ 1)]), jnp.stack([g, g ^ 1, 3 - g, 3 - (g ^ 1)])]
    )

    def first_round(low, high):
        return lax.ppermute(low, "grp", near), lax.ppermute(high, "grp", far)

    def forwarded(keep, came):
        return [(keep[e, quarter:].astype(F32) + came[e][quarter:].astype(F32)).astype(BF16) for e in range(2)]

    def second_round(low, high):
        return lax.ppermute(low, "grp", far), lax.ppermute(high, "grp", near)

    def completed(keep, came, last_came):
        return [
            (keep[e, :quarter].astype(F32) + came[e][:quarter].astype(F32) + last_came[e].astype(F32)).astype(BF16)
            for e in range(2)
        ]

    def wanted(mine):
        out = []
        for d in range(groups):
            which = lax.dynamic_index_in_dim(held, (my_group + d) % groups, 0, keepdims=False)
            out.append(jnp.where(which == 0, mine[0], mine[1]))
        return out

    def hop(sends, d):
        return lax.ppermute(sends[d], "grp", hops[d]) if d else sends[0]

    sources = jnp.stack([(my_group + groups - d) % groups for d in range(groups)]).astype(jnp.int32)

    codes_t = codes.T
    first = send_first(codes_t, flat, prob.reshape(1, tok * top), act, grad_out, columns, CHUNKS[0])
    got = {0: exchange(first)}
    outs = send_rest(codes_t, grad_out, columns, CHUNKS[0], CHUNKS[1:])
    got[0], outs = tie(got[0], outs)
    outs = dict(enumerate(outs, 1))

    starts = [sum(CHUNKS[:c]) for c in range(last + 1)]
    sends, blocks = {}, {}
    state = None
    barrier = lax.optimization_barrier
    for c in range(last + 1):
        if c == 0:
            acts, keep, low, high = weight_first(order, got[0], hidden, CHUNKS[0])
        else:
            got[c], sends[c - 1] = barrier((got[c], sends[c - 1]))
            keep, low, high = weight_rest(acts, got[c], CHUNKS[c])
            pre = lax.ppermute(sends[c - 1][2], "grp", hops[2])
            low, high, pre = barrier((low, high, pre))
            blocks[c - 1] = [sends[c - 1][0], hop(sends[c - 1], 1), pre, hop(sends[c - 1], 3)]
        if c < last:
            got[c + 1] = exchange(outs[c + 1])
            skip = act_parts if c == 0 else 0
            state = project(got[c], down_weight, starts[c], skip, CHUNKS[c], state, False)
        came = first_round(low, high)
        if c == last:
            proj = project(got[last], down_weight, starts[last], 0, CHUNKS[last], state, True)
            back = exchange(proj)
            grad_act, grad_prob = finish(codes.reshape(tok * top, 1), prob.reshape(tok * top, 1), act, back)
        if c >= 1:
            came, blocks[c - 1] = barrier((came, blocks[c - 1]))
        if c == last - 1:
            came, state = barrier((came, state))
        passed = forwarded(keep, came)
        last_came = second_round(*passed)
        if c == last:
            last_came, grad_act, grad_prob = barrier((last_came, grad_act, grad_prob))
        sends[c] = wanted(completed(keep, came, last_came))
    blocks[last] = [hop(sends[last], d) for d in range(groups)]
    own = None
    for c in range(last + 1):
        own = place(sources, blocks[c], own, hidden, width, starts[c] * V)
    return (
        grad_act.reshape(tok, top, hidden),
        grad_prob.reshape(tok, top),
        own.reshape(1, 1, hidden, width),
    )


def solution(mesh):
    placed = (
        P(("grp", "sp"), None),
        P(("grp", "sp"), None),
        P(("grp", "sp"), None),
        P(("grp", "sp"), None, None),
        P(),
        P("sp", None, None),
    )
    return jax.shard_map(
        shards,
        mesh=mesh,
        in_specs=placed,
        out_specs=(
            P(("grp", "sp"), None, None),
            P(("grp", "sp"), None),
            P("grp", "sp", None, None),
        ),
        check_vma=False,
    )
```

```python
import functools

import jax
import jax.numpy as jnp
from jax import lax
from jax.experimental import pallas as pl
from jax.experimental.pallas import tpu as pltpu
from jax.sharding import PartitionSpec as P

V = 256
MAIN = 32
LANES = 128
SHIFT = 6
MASK = (1 << SHIFT) - 1
CHUNKS = (4, 6, 6)
BF16 = jnp.bfloat16
F32 = jnp.float32
MIB = 1024 * 1024


def tie(first, second):
    return lax.optimization_barrier((first, second))


def dot(a, b, dims=((1,), (0,))):
    return lax.dot_general(a, b, (dims, ((), ())), preferred_element_type=F32)


def cost(flops, bytes_accessed):
    return pl.CostEstimate(flops=int(flops), bytes_accessed=int(bytes_accessed), transcendentals=0)


def params(mib):
    return pltpu.CompilerParams(vmem_limit_bytes=mib * MIB)


def resident():
    return pl.BlockSpec(memory_space=pltpu.VMEM)


def in_hbm(x):
    return pltpu.with_memory_space_constraint(x, pltpu.HBM)


def whole(shape):
    return pl.BlockSpec(shape, lambda *_: (0,) * len(shape))


def tail_size(n):
    return (2 * n + 7) // 8 * 8


def block_rows(n):
    return MAIN * n + tail_size(n)


SEND_STEP = 8


def main_ids(first, rows):
    i = lax.broadcasted_iota(jnp.int32, (rows, 1), 0)
    return ((first + i // MAIN) << SHIFT) + i % MAIN


def tail_ids(first, size, part):
    i = lax.broadcasted_iota(jnp.int32, (SEND_STEP * size, 1), 0)
    r = i % size
    return jnp.where(r // 2 == part, ((first + i // size) << SHIFT) + MAIN + r % 2, -1)


def hits(ids, codes):
    found = ids == codes[0:1, :]
    for k in range(1, codes.shape[0]):
        found = found | (ids == codes[k : k + 1, :])
    return jnp.where(found, 1.0, 0.0).astype(BF16)


def store_main(out_ref, part, values):
    out_ref[:, part * MAIN : (part + 1) * MAIN, :] = values.astype(BF16).reshape(SEND_STEP, MAIN, V)


def send_first_kernel(codes_ref, flat_ref, prob_ref, act_ref, grad_ref, out_ref):
    first = pl.program_id(0) * SEND_STEP
    codes, flat, prob = codes_ref[...], flat_ref[...], prob_ref[...]
    ids = main_ids(first, SEND_STEP * MAIN)
    pick = jnp.where(ids == flat, prob, 0.0).astype(BF16)
    act_parts = act_ref.shape[1] // V
    grad = grad_ref[...]
    parts = grad.shape[1] // V
    size = tail_size(act_parts + parts)
    tail = jnp.zeros((SEND_STEP * size, V), F32)
    for p in range(act_parts):
        act = act_ref[:, p * V : (p + 1) * V]
        store_main(out_ref, p, dot(pick, act))
        tail += dot(jnp.where(tail_ids(first, size, p) == flat, prob, 0.0).astype(BF16), act)
    grads = hits(ids, codes)
    for p in range(parts):
        part = grad[:, p * V : (p + 1) * V]
        store_main(out_ref, act_parts + p, dot(grads, part))
        tail += dot(hits(tail_ids(first, size, act_parts + p), codes), part)
    out_ref[:, out_ref.shape[1] - size :, :] = tail.astype(BF16).reshape(SEND_STEP, size, V)


def send_kernel(start, chunks, codes_ref, grad_ref, *out_refs):
    first = pl.program_id(0) * SEND_STEP
    codes = codes_ref[...]
    grads = hits(main_ids(first, SEND_STEP * MAIN), codes)
    at = start * V
    for n, out_ref in zip(chunks, out_refs):
        size = tail_size(n)
        tail = jnp.zeros((SEND_STEP * size, V), F32)
        for p in range(n):
            part = grad_ref[:, at : at + V]
            store_main(out_ref, p, dot(grads, part))
            tail += dot(hits(tail_ids(first, size, p), codes), part)
            at += V
        out_ref[:, MAIN * n :, :] = tail.astype(BF16).reshape(SEND_STEP, size, V)


def send_first(codes, flat, prob, act, grad, columns, parts):
    routes, hidden = act.shape
    tok = grad.shape[0]
    rows = block_rows(hidden // V + parts)
    return pl.pallas_call(
        send_first_kernel,
        grid=(columns // SEND_STEP,),
        in_specs=[
            whole(codes.shape),
            whole(flat.shape),
            whole(prob.shape),
            whole(act.shape),
            pl.BlockSpec((tok, parts * V), lambda i: (0, 0)),
        ],
        out_specs=pl.BlockSpec((SEND_STEP, rows, V), lambda i: (i, 0, 0)),
        out_shape=pltpu.HBM((columns, rows, V), BF16),
        compiler_params=params(24),
        cost_estimate=cost(2 * columns * MAIN * routes * hidden, 2 * columns * rows * V + 2 * routes * hidden),
        name="send_first",
    )(codes, flat, prob, in_hbm(act), in_hbm(grad))


def send_rest(codes, grad, columns, start, chunks):
    tok, width = grad.shape
    shapes = [(columns, block_rows(n), V) for n in chunks]
    return pl.pallas_call(
        functools.partial(send_kernel, start, chunks),
        grid=(columns // SEND_STEP,),
        in_specs=[whole(codes.shape), whole(grad.shape)],
        out_specs=[pl.BlockSpec((SEND_STEP, s[1], V), lambda i: (i, 0, 0)) for s in shapes],
        out_shape=[pltpu.HBM(s, BF16) for s in shapes],
        compiler_params=params(24),
        cost_estimate=cost(2 * columns * MAIN * tok * width, 2 * columns * 34 * width + 2 * tok * width),
        name="send_rest",
    )(codes, in_hbm(grad))


def load_tail(got_ref, tail_ref):
    sources, rows, _ = got_ref.shape
    n = rows // MAIN
    for h in range(V // LANES):
        part = got_ref[:, n * MAIN :, h * LANES : (h + 1) * LANES].astype(F32)
        tail_ref[h] = part.reshape(tail_ref.shape[1:])


def tail_rows(tail_ref, sources, part, expert):
    size = tail_ref.shape[1] // sources
    rows = [tail_ref[h, pl.ds(2 * part + expert, sources, stride=size), :] for h in range(V // LANES)]
    return jnp.concatenate(rows, axis=1).astype(BF16)


def main_rows(got_ref, part, expert):
    half = MAIN // 2
    rows = got_ref[:, pl.ds(part * MAIN + expert * half, half), :]
    return rows.reshape(got_ref.shape[0] * half, V)


def parts_a_step(parts):
    return parts // 2 if parts % 2 == 0 else parts


def weight_step(acts, got_ref, tail_ref, part, count, keep_ref, send_ref, expert):
    sources = got_ref.shape[0]
    rows = jnp.concatenate([main_rows(got_ref, part + i, expert) for i in range(count)], axis=1)
    more = jnp.concatenate([tail_rows(tail_ref, sources, part + i, expert) for i in range(count)], axis=1)
    total = dot(acts, jnp.concatenate([rows, more], axis=0))
    half = total.shape[0] // 2
    size = count * V
    at = pl.multiple_of(pl.program_id(0) * size, size)
    keep_ref[expert, :, pl.ds(at, size)] = total[:half].astype(BF16)
    send_ref[:, pl.ds(at, size)] = total[half:].astype(BF16)


def weight_first_kernel(act_parts, order_ref, got_ref, acts_ref, keep_ref, low_ref, high_ref, tail_ref, plain_ref):
    sources = got_ref.shape[0]
    part = pl.program_id(0)

    @pl.when(part == 0)
    def _():
        load_tail(got_ref, tail_ref)
        quarters = order_ref.shape[1]
        size = acts_ref.shape[1] // quarters
        for e in range(2):
            for p in range(act_parts):
                block = main_rows(got_ref, p, e)
                more = tail_rows(tail_ref, sources, p, e)
                plain_ref[p * V : (p + 1) * V, : block.shape[0]] = block.astype(F32).T.astype(BF16)
                plain_ref[p * V : (p + 1) * V, block.shape[0] :] = more.astype(F32).T.astype(BF16)
            for q in range(quarters):
                at = pl.multiple_of(order_ref[e, q] * size, size)
                acts_ref[e, q * size : (q + 1) * size, :] = plain_ref[pl.ds(at, size), :]

    count = parts_a_step(low_ref.shape[1] // V)
    for e, send_ref in enumerate((low_ref, high_ref)):
        weight_step(acts_ref[e], got_ref, tail_ref, act_parts + part * count, count, keep_ref, send_ref, e)


def weight_kernel(acts_ref, got_ref, keep_ref, low_ref, high_ref, tail_ref):
    part = pl.program_id(0)

    @pl.when(part == 0)
    def _():
        load_tail(got_ref, tail_ref)

    count = parts_a_step(low_ref.shape[1] // V)
    for e, send_ref in enumerate((low_ref, high_ref)):
        weight_step(acts_ref[e], got_ref, tail_ref, part * count, count, keep_ref, send_ref, e)


def sum_specs(hidden, parts):
    half = hidden // 2
    specs = [resident()] * 3
    shapes = [jax.ShapeDtypeStruct(s, BF16) for s in ((2, half, parts * V), (half, parts * V), (half, parts * V))]
    return specs, shapes


def tail_scratch(got):
    return pltpu.VMEM((V // LANES, got.shape[0] * (got.shape[1] % MAIN), LANES), F32)


def weight_first(order, got, hidden, parts):
    depth = got.shape[0] * (MAIN // 2 + 1)
    specs, shapes = sum_specs(hidden, parts)
    return pl.pallas_call(
        functools.partial(weight_first_kernel, hidden // V),
        grid=(parts // parts_a_step(parts),),
        in_specs=[pl.BlockSpec(memory_space=pltpu.SMEM), resident()],
        out_specs=[whole((2, hidden, depth))] + specs,
        out_shape=[pltpu.HBM((2, hidden, depth), BF16)] + shapes,
        scratch_shapes=[tail_scratch(got), pltpu.VMEM((hidden, depth), BF16)],
        compiler_params=params(16),
        cost_estimate=cost(4 * depth * hidden * V * parts, 2 * (got.size + 4 * depth * hidden)),
        name="weight_first",
    )(order, got)


def weight_rest(acts, got, parts):
    hidden, depth = acts.shape[1:]
    specs, shapes = sum_specs(hidden, parts)
    return pl.pallas_call(
        weight_kernel,
        grid=(parts // parts_a_step(parts),),
        in_specs=[whole(acts.shape), resident()],
        out_specs=specs,
        out_shape=shapes,
        scratch_shapes=[tail_scratch(got)],
        compiler_params=params(16),
        cost_estimate=cost(4 * depth * hidden * V * parts, 2 * (got.size + acts.size + 2 * hidden * V * parts)),
        name="weight_rest",
    )(in_hbm(acts), got)


def project_kernel(skip, parts, chained, final, *refs):
    refs = list(refs)
    got_ref, weight_ref = refs[:2]
    refs = refs[2:]
    if chained:
        main_in, tail_in = refs[:2]
        refs = refs[2:]
    if final:
        out_ref, main_acc, tail_acc, tail_ref = refs
    else:
        main_acc, tail_acc, tail_ref = refs
    sources = got_ref.shape[0]
    half = MAIN // 2
    part = pl.program_id(0)

    @pl.when(part == 0)
    def _():
        load_tail(got_ref, tail_ref)
        if chained:
            main_acc[...] = main_in[...]
            tail_acc[...] = tail_in[...]
        else:
            main_acc[...] = jnp.zeros_like(main_acc)
            tail_acc[...] = jnp.zeros_like(tail_acc)

    for e in range(2):
        weight = weight_ref[e]
        rows = main_rows(got_ref, part + skip, e)
        main_acc[e] += dot(rows, weight, ((1,), (1,)))
        more = tail_rows(tail_ref, sources, part + skip, e)
        tail_acc[e] += dot(more, weight, ((1,), (1,)))

    if final:

        @pl.when(part == parts - 1)
        def _():
            hidden = weight_ref.shape[1]
            n = hidden // V
            rows = tail_size(n)
            size = sources * rows
            i = lax.broadcasted_iota(jnp.int32, (size, sources), 0)
            j = lax.broadcasted_iota(jnp.int32, (size, sources), 1)
            tail = jnp.zeros((size, V), F32)
            for e in range(2):
                for p in range(n):
                    block = main_acc[e, :, p * V : (p + 1) * V].astype(BF16)
                    at = p * MAIN + e * half
                    out_ref[:, at : at + half, :] = block.reshape(sources, half, V)
                    order = (i // rows == j) & (i % rows == 2 * p + e)
                    more = tail_acc[e, :, p * V : (p + 1) * V].astype(BF16)
                    tail += dot(jnp.where(order, 1.0, 0.0).astype(BF16), more)
            out_ref[:, n * MAIN :, :] = tail.reshape(sources, rows, V).astype(BF16)


def project(got, weight, at, skip, parts, state, final):
    sources = got.shape[0]
    hidden = weight.shape[1]
    half = MAIN // 2
    main_shape, tail_shape = (2, sources * half, hidden), (2, sources, hidden)
    in_specs = [resident(), pl.BlockSpec((2, hidden, V), lambda p: (0, 0, at + p))]
    args = [got, in_hbm(weight)]
    if state is not None:
        in_specs += [resident(), resident()]
        args += list(state)
    scratch = [pltpu.VMEM((V // LANES, sources * (got.shape[1] % MAIN), LANES), F32)]
    if final:
        shape = (sources, block_rows(hidden // V), V)
        out_specs, out_shape = resident(), jax.ShapeDtypeStruct(shape, BF16)
        scratch = [pltpu.VMEM(main_shape, F32), pltpu.VMEM(tail_shape, F32)] + scratch
    else:
        out_specs = [resident(), resident()]
        out_shape = [jax.ShapeDtypeStruct(main_shape, F32), jax.ShapeDtypeStruct(tail_shape, F32)]
    return pl.pallas_call(
        functools.partial(project_kernel, skip, parts, state is not None, final),
        grid=(parts,),
        in_specs=in_specs,
        out_specs=out_specs,
        out_shape=out_shape,
        scratch_shapes=scratch,
        compiler_params=params(20),
        cost_estimate=cost(4 * sources * 17 * hidden * V * parts, 2 * got.size + 4 * hidden * V * parts + 16 * sources * 17 * hidden),
        name="project",
    )(*args)


FINISH_STEP = 256


def finish_kernel(code_ref, prob_ref, act_ref, back_ref, grad_act_ref, grad_prob_ref):
    code = code_ref[...]
    column, row = code >> SHIFT, code & MASK
    sources = back_ref.shape[0]
    hidden = act_ref.shape[1]
    n = hidden // V
    steps = code.shape[0]
    main_id = jnp.where(row < MAIN, column * MAIN + row, -1)
    lanes = lax.broadcasted_iota(jnp.int32, (steps, sources * MAIN), 1)
    pick = jnp.where(lanes == main_id, 1.0, 0.0).astype(BF16)
    rows = tail_size(n)
    tail = back_ref[:, n * MAIN :, :].astype(F32).reshape(sources * rows, V).astype(BF16)
    lanes = lax.broadcasted_iota(jnp.int32, (steps, sources * rows), 1)
    prob = prob_ref[...]
    total = jnp.zeros((steps, 1), F32)
    for p in range(n):
        main = back_ref[:, p * MAIN : (p + 1) * MAIN, :].reshape(sources * MAIN, V)
        tail_id = jnp.where(row >= MAIN, column * rows + 2 * p + (row - MAIN), -1)
        proj = dot(pick, main) + dot(jnp.where(lanes == tail_id, 1.0, 0.0).astype(BF16), tail)
        act = act_ref[:, p * V : (p + 1) * V].astype(F32)
        total += jnp.sum(act * proj, axis=1, keepdims=True)
        grad_act_ref[:, p * V : (p + 1) * V] = (prob * proj).astype(BF16)
    grad_prob_ref[...] = total


def finish(code, prob, act, back):
    routes, hidden = act.shape
    one = pl.BlockSpec((FINISH_STEP, 1), lambda i: (i, 0))
    rows = pl.BlockSpec((FINISH_STEP, hidden), lambda i: (i, 0))
    return pl.pallas_call(
        finish_kernel,
        grid=(routes // FINISH_STEP,),
        in_specs=[one, one, rows, resident()],
        out_specs=[rows, one],
        out_shape=[jax.ShapeDtypeStruct((routes, hidden), BF16), jax.ShapeDtypeStruct((routes, 1), F32)],
        compiler_params=params(24),
        cost_estimate=cost(2 * routes * routes * hidden, 2 * (back.size + 2 * routes * hidden)),
        name="finish",
    )(code, prob, act, back)


def place_kernel(column, sources_ref, *refs):
    blocks, (out_ref, sems) = refs[:4], refs[-2:]
    copies = []
    for d, block in enumerate(blocks):
        rows, size = block.shape
        row = pl.multiple_of(sources_ref[d] * rows, rows)
        copies.append(
            pltpu.make_async_copy(block, out_ref.at[pl.ds(row, rows), pl.ds(column, size)], sems.at[d])
        )
    for copy in copies:
        copy.start()
    for copy in copies:
        copy.wait()


def place(sources, blocks, own, hidden, width, column):
    first = own is None
    args = [sources, *blocks] + ([] if first else [own])
    own_spec = pl.BlockSpec(memory_space=pltpu.HBM)
    return pl.pallas_call(
        functools.partial(place_kernel, column),
        in_specs=[pl.BlockSpec(memory_space=pltpu.SMEM)] + [resident()] * len(blocks) + [own_spec] * (not first),
        out_specs=own_spec,
        out_shape=pltpu.HBM((hidden, width), BF16),
        scratch_shapes=[pltpu.SemaphoreType.DMA((len(blocks),))],
        input_output_aliases={} if first else {len(args) - 1: 0},
        compiler_params=params(4),
        cost_estimate=cost(0, 4 * hidden * blocks[0].shape[1]),
        name="place",
    )(*args)


def route_codes(routes, columns):
    tok, top = routes.shape
    experts = 2 * columns
    base = MAIN // 2
    hit = routes[:, :, None] == jnp.arange(experts)[None, None, :]
    member = jnp.any(hit, axis=1).astype(BF16)
    lower = (jnp.arange(tok)[:, None] > jnp.arange(tok)[None, :]).astype(BF16)
    rank = dot(lower, member)
    rank = jnp.sum(jnp.where(hit, rank[:, None, :], 0.0), axis=2).astype(jnp.int32)
    low = routes % 2
    row = jnp.where(rank < base, low * base + rank, MAIN + low)
    return ((routes // 2) << SHIFT) + row


def shards(grad_out, routes, probs, hidden_act, placement, down_weight):
    groups = lax.axis_size("grp")
    columns = lax.axis_size("sp")
    my_group = lax.axis_index("grp")
    my_column = lax.axis_index("sp")
    tok, width = grad_out.shape
    top = routes.shape[1]
    hidden = hidden_act.shape[2]
    quarter = hidden // groups
    act_parts = hidden // V
    last = len(CHUNKS) - 1

    codes = route_codes(routes, columns)
    flat = codes.reshape(1, tok * top)
    prob = probs.astype(F32)
    act = hidden_act.reshape(tok * top, hidden)

    def exchange(v):
        return lax.all_to_all(v, "sp", 0, 0, tiled=True)

    held = lax.dynamic_index_in_dim(placement, my_column, 1, keepdims=False) - 2 * my_column
    hops = [[(i, (i + d) % groups) for i in range(groups)] for d in range(groups)]

    near = [(0, 1), (1, 0), (2, 3), (3, 2)]
    far = [(0, 3), (3, 0), (1, 2), (2, 1)]
    g = my_group.astype(jnp.int32)
    order = jnp.stack(
        [jnp.stack([g, 3 - g, g ^ 1, 3 - (g ^ 1)]), jnp.stack([g, g ^ 1, 3 - g, 3 - (g ^ 1)])]
    )

    def first_round(low, high):
        return lax.ppermute(low, "grp", near), lax.ppermute(high, "grp", far)

    def forwarded(keep, came):
        return [(keep[e, quarter:].astype(F32) + came[e][quarter:].astype(F32)).astype(BF16) for e in range(2)]

    def second_round(low, high):
        return lax.ppermute(low, "grp", far), lax.ppermute(high, "grp", near)

    def completed(keep, came, last_came):
        return [
            (keep[e, :quarter].astype(F32) + came[e][:quarter].astype(F32) + last_came[e].astype(F32)).astype(BF16)
            for e in range(2)
        ]

    def wanted(mine):
        out = []
        for d in range(groups):
            which = lax.dynamic_index_in_dim(held, (my_group + d) % groups, 0, keepdims=False)
            out.append(jnp.where(which == 0, mine[0], mine[1]))
        return out

    def hop(sends, d):
        return lax.ppermute(sends[d], "grp", hops[d]) if d else sends[0]

    sources = jnp.stack([(my_group + groups - d) % groups for d in range(groups)]).astype(jnp.int32)

    codes_t = codes.T
    first = send_first(codes_t, flat, prob.reshape(1, tok * top), act, grad_out, columns, CHUNKS[0])
    got = {0: exchange(first)}
    outs = send_rest(codes_t, grad_out, columns, CHUNKS[0], CHUNKS[1:])
    got[0], outs = tie(got[0], outs)
    outs = dict(enumerate(outs, 1))

    starts = [sum(CHUNKS[:c]) for c in range(last + 1)]
    sends, blocks = {}, {}
    state = None
    barrier = lax.optimization_barrier
    for c in range(last + 1):
        if c == 0:
            acts, keep, low, high = weight_first(order, got[0], hidden, CHUNKS[0])
        else:
            got[c], sends[c - 1] = barrier((got[c], sends[c - 1]))
            keep, low, high = weight_rest(acts, got[c], CHUNKS[c])
            pre = lax.ppermute(sends[c - 1][2], "grp", hops[2])
            low, high, pre = barrier((low, high, pre))
            blocks[c - 1] = [sends[c - 1][0], hop(sends[c - 1], 1), pre, hop(sends[c - 1], 3)]
        if c < last:
            got[c + 1] = exchange(outs[c + 1])
            skip = act_parts if c == 0 else 0
            state = project(got[c], down_weight, starts[c], skip, CHUNKS[c], state, False)
        came = first_round(low, high)
        if c == last:
            proj = project(got[last], down_weight, starts[last], 0, CHUNKS[last], state, True)
            back = exchange(proj)
            grad_act, grad_prob = finish(code_column, prob_column, act, back)
        if c >= 1:
            came, blocks[c - 1] = barrier((came, blocks[c - 1]))
        if c == last - 1:
            came, state, code_column, prob_column = barrier(
                (came, state, codes.reshape(tok * top, 1), prob.reshape(tok * top, 1))
            )
        passed = forwarded(keep, came)
        last_came = second_round(*passed)
        if c == last:
            last_came, grad_act, grad_prob = barrier((last_came, grad_act, grad_prob))
        sends[c] = wanted(completed(keep, came, last_came))
    blocks[last] = [hop(sends[last], d) for d in range(groups)]
    own = None
    for c in range(last + 1):
        own = place(sources, blocks[c], own, hidden, width, starts[c] * V)
    return (
        grad_act.reshape(tok, top, hidden),
        grad_prob.reshape(tok, top),
        own.reshape(1, 1, hidden, width),
    )


def solution(mesh):
    placed = (
        P(("grp", "sp"), None),
        P(("grp", "sp"), None),
        P(("grp", "sp"), None),
        P(("grp", "sp"), None, None),
        P(),
        P("sp", None, None),
    )
    return jax.shard_map(
        shards,
        mesh=mesh,
        in_specs=placed,
        out_specs=(
            P(("grp", "sp"), None, None),
            P(("grp", "sp"), None),
            P("grp", "sp", None, None),
        ),
        check_vma=False,
    )
```

```python
import functools

import jax
import jax.numpy as jnp
from jax import lax
from jax.experimental import pallas as pl
from jax.experimental.pallas import tpu as pltpu
from jax.sharding import PartitionSpec as P

V = 256
MAIN = 32
LANES = 128
SHIFT = 6
MASK = (1 << SHIFT) - 1
CHUNKS = (4, 6, 6)
BF16 = jnp.bfloat16
F32 = jnp.float32
MIB = 1024 * 1024


def tie(first, second):
    return lax.optimization_barrier((first, second))


def dot(a, b, dims=((1,), (0,))):
    return lax.dot_general(a, b, (dims, ((), ())), preferred_element_type=F32)


def cost(flops, bytes_accessed):
    return pl.CostEstimate(flops=int(flops), bytes_accessed=int(bytes_accessed), transcendentals=0)


def params(mib):
    return pltpu.CompilerParams(vmem_limit_bytes=mib * MIB)


def resident():
    return pl.BlockSpec(memory_space=pltpu.VMEM)


def in_hbm(x):
    return pltpu.with_memory_space_constraint(x, pltpu.HBM)


def whole(shape):
    return pl.BlockSpec(shape, lambda *_: (0,) * len(shape))


def tail_size(n):
    return (2 * n + 7) // 8 * 8


def block_rows(n):
    return MAIN * n + tail_size(n)


SEND_STEP = 8


def main_ids(first, rows):
    i = lax.broadcasted_iota(jnp.int32, (rows, 1), 0)
    return ((first + i // MAIN) << SHIFT) + i % MAIN


def tail_ids(first, size, part):
    i = lax.broadcasted_iota(jnp.int32, (SEND_STEP * size, 1), 0)
    r = i % size
    return jnp.where(r // 2 == part, ((first + i // size) << SHIFT) + MAIN + r % 2, -1)


def hits(ids, codes):
    found = ids == codes[0:1, :]
    for k in range(1, codes.shape[0]):
        found = found | (ids == codes[k : k + 1, :])
    return jnp.where(found, 1.0, 0.0).astype(BF16)


def store_main(out_ref, part, values):
    out_ref[:, part * MAIN : (part + 1) * MAIN, :] = values.astype(BF16).reshape(SEND_STEP, MAIN, V)


def send_first_kernel(codes_ref, flat_ref, prob_ref, act_ref, grad_ref, out_ref):
    first = pl.program_id(0) * SEND_STEP
    codes, flat, prob = codes_ref[...], flat_ref[...], prob_ref[...]
    ids = main_ids(first, SEND_STEP * MAIN)
    pick = jnp.where(ids == flat, prob, 0.0).astype(BF16)
    act_parts = act_ref.shape[1] // V
    grad = grad_ref[...]
    parts = grad.shape[1] // V
    size = tail_size(act_parts + parts)
    tail = jnp.zeros((SEND_STEP * size, V), F32)
    for p in range(act_parts):
        act = act_ref[:, p * V : (p + 1) * V]
        store_main(out_ref, p, dot(pick, act))
        tail += dot(jnp.where(tail_ids(first, size, p) == flat, prob, 0.0).astype(BF16), act)
    grads = hits(ids, codes)
    for p in range(parts):
        part = grad[:, p * V : (p + 1) * V]
        store_main(out_ref, act_parts + p, dot(grads, part))
        tail += dot(hits(tail_ids(first, size, act_parts + p), codes), part)
    out_ref[:, out_ref.shape[1] - size :, :] = tail.astype(BF16).reshape(SEND_STEP, size, V)


def send_kernel(start, chunks, codes_ref, grad_ref, *out_refs):
    first = pl.program_id(0) * SEND_STEP
    codes = codes_ref[...]
    grads = hits(main_ids(first, SEND_STEP * MAIN), codes)
    at = start * V
    for n, out_ref in zip(chunks, out_refs):
        size = tail_size(n)
        tail = jnp.zeros((SEND_STEP * size, V), F32)
        for p in range(n):
            part = grad_ref[:, at : at + V]
            store_main(out_ref, p, dot(grads, part))
            tail += dot(hits(tail_ids(first, size, p), codes), part)
            at += V
        out_ref[:, MAIN * n :, :] = tail.astype(BF16).reshape(SEND_STEP, size, V)


def send_first(codes, flat, prob, act, grad, columns, parts):
    routes, hidden = act.shape
    tok = grad.shape[0]
    rows = block_rows(hidden // V + parts)
    return pl.pallas_call(
        send_first_kernel,
        grid=(columns // SEND_STEP,),
        in_specs=[
            whole(codes.shape),
            whole(flat.shape),
            whole(prob.shape),
            whole(act.shape),
            pl.BlockSpec((tok, parts * V), lambda i: (0, 0)),
        ],
        out_specs=pl.BlockSpec((SEND_STEP, rows, V), lambda i: (i, 0, 0)),
        out_shape=pltpu.HBM((columns, rows, V), BF16),
        compiler_params=params(24),
        cost_estimate=cost(2 * columns * MAIN * routes * hidden, 2 * columns * rows * V + 2 * routes * hidden),
        name="send_first",
    )(codes, flat, prob, in_hbm(act), in_hbm(grad))


def send_rest(codes, grad, columns, start, chunks):
    tok, width = grad.shape
    shapes = [(columns, block_rows(n), V) for n in chunks]
    return pl.pallas_call(
        functools.partial(send_kernel, start, chunks),
        grid=(columns // SEND_STEP,),
        in_specs=[whole(codes.shape), whole(grad.shape)],
        out_specs=[pl.BlockSpec((SEND_STEP, s[1], V), lambda i: (i, 0, 0)) for s in shapes],
        out_shape=[pltpu.HBM(s, BF16) for s in shapes],
        compiler_params=params(24),
        cost_estimate=cost(2 * columns * MAIN * tok * width, 2 * columns * 34 * width + 2 * tok * width),
        name="send_rest",
    )(codes, in_hbm(grad))


def load_tail(got_ref, tail_ref):
    sources, rows, _ = got_ref.shape
    n = rows // MAIN
    for h in range(V // LANES):
        part = got_ref[:, n * MAIN :, h * LANES : (h + 1) * LANES].astype(F32)
        tail_ref[h] = part.reshape(tail_ref.shape[1:])


def tail_rows(tail_ref, sources, part, expert):
    size = tail_ref.shape[1] // sources
    rows = [tail_ref[h, pl.ds(2 * part + expert, sources, stride=size), :] for h in range(V // LANES)]
    return jnp.concatenate(rows, axis=1).astype(BF16)


def main_rows(got_ref, part, expert):
    half = MAIN // 2
    rows = got_ref[:, pl.ds(part * MAIN + expert * half, half), :]
    return rows.reshape(got_ref.shape[0] * half, V)


def parts_a_step(parts):
    return parts // 2 if parts % 2 == 0 else parts


def weight_step(acts, got_ref, tail_ref, part, count, keep_ref, send_ref, expert):
    sources = got_ref.shape[0]
    rows = jnp.concatenate([main_rows(got_ref, part + i, expert) for i in range(count)], axis=1)
    more = jnp.concatenate([tail_rows(tail_ref, sources, part + i, expert) for i in range(count)], axis=1)
    total = dot(acts, jnp.concatenate([rows, more], axis=0))
    half = total.shape[0] // 2
    size = count * V
    at = pl.multiple_of(pl.program_id(0) * size, size)
    keep_ref[expert, :, pl.ds(at, size)] = total[:half].astype(BF16)
    send_ref[:, pl.ds(at, size)] = total[half:].astype(BF16)


def weight_first_kernel(act_parts, order_ref, got_ref, acts_ref, keep_ref, low_ref, high_ref, tail_ref, plain_ref):
    sources = got_ref.shape[0]
    part = pl.program_id(0)

    @pl.when(part == 0)
    def _():
        load_tail(got_ref, tail_ref)
        quarters = order_ref.shape[1]
        size = acts_ref.shape[1] // quarters
        for e in range(2):
            for p in range(act_parts):
                block = main_rows(got_ref, p, e)
                more = tail_rows(tail_ref, sources, p, e)
                plain_ref[p * V : (p + 1) * V, : block.shape[0]] = block.astype(F32).T.astype(BF16)
                plain_ref[p * V : (p + 1) * V, block.shape[0] :] = more.astype(F32).T.astype(BF16)
            for q in range(quarters):
                at = pl.multiple_of(order_ref[e, q] * size, size)
                acts_ref[e, q * size : (q + 1) * size, :] = plain_ref[pl.ds(at, size), :]

    count = parts_a_step(low_ref.shape[1] // V)
    for e, send_ref in enumerate((low_ref, high_ref)):
        weight_step(acts_ref[e], got_ref, tail_ref, act_parts + part * count, count, keep_ref, send_ref, e)


def weight_kernel(acts_ref, got_ref, keep_ref, low_ref, high_ref, tail_ref):
    part = pl.program_id(0)

    @pl.when(part == 0)
    def _():
        load_tail(got_ref, tail_ref)

    count = parts_a_step(low_ref.shape[1] // V)
    for e, send_ref in enumerate((low_ref, high_ref)):
        weight_step(acts_ref[e], got_ref, tail_ref, part * count, count, keep_ref, send_ref, e)


def sum_specs(hidden, parts):
    half = hidden // 2
    specs = [resident()] * 3
    shapes = [jax.ShapeDtypeStruct(s, BF16) for s in ((2, half, parts * V), (half, parts * V), (half, parts * V))]
    return specs, shapes


def tail_scratch(got):
    return pltpu.VMEM((V // LANES, got.shape[0] * (got.shape[1] % MAIN), LANES), F32)


def weight_first(order, got, hidden, parts):
    depth = got.shape[0] * (MAIN // 2 + 1)
    specs, shapes = sum_specs(hidden, parts)
    return pl.pallas_call(
        functools.partial(weight_first_kernel, hidden // V),
        grid=(parts // parts_a_step(parts),),
        in_specs=[pl.BlockSpec(memory_space=pltpu.SMEM), resident()],
        out_specs=[whole((2, hidden, depth))] + specs,
        out_shape=[pltpu.HBM((2, hidden, depth), BF16)] + shapes,
        scratch_shapes=[tail_scratch(got), pltpu.VMEM((hidden, depth), BF16)],
        compiler_params=params(16),
        cost_estimate=cost(4 * depth * hidden * V * parts, 2 * (got.size + 4 * depth * hidden)),
        name="weight_first",
    )(order, got)


def weight_rest(acts, got, parts):
    hidden, depth = acts.shape[1:]
    specs, shapes = sum_specs(hidden, parts)
    return pl.pallas_call(
        weight_kernel,
        grid=(parts // parts_a_step(parts),),
        in_specs=[whole(acts.shape), resident()],
        out_specs=specs,
        out_shape=shapes,
        scratch_shapes=[tail_scratch(got)],
        compiler_params=params(16),
        cost_estimate=cost(4 * depth * hidden * V * parts, 2 * (got.size + acts.size + 2 * hidden * V * parts)),
        name="weight_rest",
    )(in_hbm(acts), got)


def project_kernel(skip, parts, chained, final, *refs):
    refs = list(refs)
    got_ref, weight_ref = refs[:2]
    refs = refs[2:]
    if chained:
        main_in, tail_in = refs[:2]
        refs = refs[2:]
    if final:
        out_ref, main_acc, tail_acc, tail_ref = refs
    else:
        main_acc, tail_acc, tail_ref = refs
    sources = got_ref.shape[0]
    half = MAIN // 2
    part = pl.program_id(0)

    @pl.when(part == 0)
    def _():
        load_tail(got_ref, tail_ref)
        if chained:
            main_acc[...] = main_in[...]
            tail_acc[...] = tail_in[...]
        else:
            main_acc[...] = jnp.zeros_like(main_acc)
            tail_acc[...] = jnp.zeros_like(tail_acc)

    for e in range(2):
        weight = weight_ref[e]
        rows = main_rows(got_ref, part + skip, e)
        main_acc[e] += dot(rows, weight, ((1,), (1,)))
        more = tail_rows(tail_ref, sources, part + skip, e)
        tail_acc[e] += dot(more, weight, ((1,), (1,)))

    if final:

        @pl.when(part == parts - 1)
        def _():
            hidden = weight_ref.shape[1]
            n = hidden // V
            rows = tail_size(n)
            size = sources * rows
            i = lax.broadcasted_iota(jnp.int32, (size, sources), 0)
            j = lax.broadcasted_iota(jnp.int32, (size, sources), 1)
            tail = jnp.zeros((size, V), F32)
            for e in range(2):
                for p in range(n):
                    block = main_acc[e, :, p * V : (p + 1) * V].astype(BF16)
                    at = p * MAIN + e * half
                    out_ref[:, at : at + half, :] = block.reshape(sources, half, V)
                    order = (i // rows == j) & (i % rows == 2 * p + e)
                    more = tail_acc[e, :, p * V : (p + 1) * V].astype(BF16)
                    tail += dot(jnp.where(order, 1.0, 0.0).astype(BF16), more)
            out_ref[:, n * MAIN :, :] = tail.reshape(sources, rows, V).astype(BF16)


def project(got, weight, at, skip, parts, state, final):
    sources = got.shape[0]
    hidden = weight.shape[1]
    half = MAIN // 2
    main_shape, tail_shape = (2, sources * half, hidden), (2, sources, hidden)
    in_specs = [resident(), pl.BlockSpec((2, hidden, V), lambda p: (0, 0, at + p))]
    args = [got, in_hbm(weight)]
    if state is not None:
        in_specs += [resident(), resident()]
        args += list(state)
    scratch = [pltpu.VMEM((V // LANES, sources * (got.shape[1] % MAIN), LANES), F32)]
    if final:
        shape = (sources, block_rows(hidden // V), V)
        out_specs, out_shape = resident(), jax.ShapeDtypeStruct(shape, BF16)
        scratch = [pltpu.VMEM(main_shape, F32), pltpu.VMEM(tail_shape, F32)] + scratch
    else:
        out_specs = [resident(), resident()]
        out_shape = [jax.ShapeDtypeStruct(main_shape, F32), jax.ShapeDtypeStruct(tail_shape, F32)]
    return pl.pallas_call(
        functools.partial(project_kernel, skip, parts, state is not None, final),
        grid=(parts,),
        in_specs=in_specs,
        out_specs=out_specs,
        out_shape=out_shape,
        scratch_shapes=scratch,
        compiler_params=params(20),
        cost_estimate=cost(4 * sources * 17 * hidden * V * parts, 2 * got.size + 4 * hidden * V * parts + 16 * sources * 17 * hidden),
        name="project",
    )(*args)


FINISH_STEP = 256


def finish_kernel(code_ref, prob_ref, act_ref, back_ref, grad_act_ref, grad_prob_ref):
    code = code_ref[...]
    column, row = code >> SHIFT, code & MASK
    sources = back_ref.shape[0]
    hidden = act_ref.shape[1]
    n = hidden // V
    steps = code.shape[0]
    main_id = jnp.where(row < MAIN, column * MAIN + row, -1)
    lanes = lax.broadcasted_iota(jnp.int32, (steps, sources * MAIN), 1)
    pick = jnp.where(lanes == main_id, 1.0, 0.0).astype(BF16)
    rows = tail_size(n)
    tail = back_ref[:, n * MAIN :, :].astype(F32).reshape(sources * rows, V).astype(BF16)
    lanes = lax.broadcasted_iota(jnp.int32, (steps, sources * rows), 1)
    prob = prob_ref[...]
    total = jnp.zeros((steps, 1), F32)
    for p in range(n):
        main = back_ref[:, p * MAIN : (p + 1) * MAIN, :].reshape(sources * MAIN, V)
        tail_id = jnp.where(row >= MAIN, column * rows + 2 * p + (row - MAIN), -1)
        proj = dot(pick, main) + dot(jnp.where(lanes == tail_id, 1.0, 0.0).astype(BF16), tail)
        act = act_ref[:, p * V : (p + 1) * V].astype(F32)
        total += jnp.sum(act * proj, axis=1, keepdims=True)
        grad_act_ref[:, p * V : (p + 1) * V] = (prob * proj).astype(BF16)
    grad_prob_ref[...] = total


def finish(code, prob, act, back):
    routes, hidden = act.shape
    one = pl.BlockSpec((FINISH_STEP, 1), lambda i: (i, 0))
    rows = pl.BlockSpec((FINISH_STEP, hidden), lambda i: (i, 0))
    return pl.pallas_call(
        finish_kernel,
        grid=(routes // FINISH_STEP,),
        in_specs=[one, one, rows, resident()],
        out_specs=[rows, one],
        out_shape=[jax.ShapeDtypeStruct((routes, hidden), BF16), jax.ShapeDtypeStruct((routes, 1), F32)],
        compiler_params=params(24),
        cost_estimate=cost(2 * routes * routes * hidden, 2 * (back.size + 2 * routes * hidden)),
        name="finish",
    )(code, prob, act, back)


def place_kernel(column, count, sources_ref, *refs):
    blocks, (out_ref, sems) = refs[:count], refs[-2:]
    copies = []
    for d, block in enumerate(blocks):
        rows, size = block.shape
        row = pl.multiple_of(sources_ref[d] * rows, rows)
        copies.append(
            pltpu.make_async_copy(block, out_ref.at[pl.ds(row, rows), pl.ds(column, size)], sems.at[d])
        )
    for copy in copies:
        copy.start()
    for copy in copies:
        copy.wait()


def place(sources, blocks, own, hidden, width, column):
    first = own is None
    args = [sources, *blocks] + ([] if first else [own])
    own_spec = pl.BlockSpec(memory_space=pltpu.HBM)
    return pl.pallas_call(
        functools.partial(place_kernel, column, len(blocks)),
        in_specs=[pl.BlockSpec(memory_space=pltpu.SMEM)] + [resident()] * len(blocks) + [own_spec] * (not first),
        out_specs=own_spec,
        out_shape=pltpu.HBM((hidden, width), BF16),
        scratch_shapes=[pltpu.SemaphoreType.DMA((len(blocks),))],
        input_output_aliases={} if first else {len(args) - 1: 0},
        compiler_params=params(4),
        cost_estimate=cost(0, 4 * hidden * blocks[0].shape[1]),
        name="place",
    )(*args)


def route_codes(routes, columns):
    tok, top = routes.shape
    experts = 2 * columns
    base = MAIN // 2
    hit = routes[:, :, None] == jnp.arange(experts)[None, None, :]
    member = jnp.any(hit, axis=1).astype(BF16)
    lower = (jnp.arange(tok)[:, None] > jnp.arange(tok)[None, :]).astype(BF16)
    rank = dot(lower, member)
    rank = jnp.sum(jnp.where(hit, rank[:, None, :], 0.0), axis=2).astype(jnp.int32)
    low = routes % 2
    row = jnp.where(rank < base, low * base + rank, MAIN + low)
    return ((routes // 2) << SHIFT) + row


def shards(grad_out, routes, probs, hidden_act, placement, down_weight):
    groups = lax.axis_size("grp")
    columns = lax.axis_size("sp")
    my_group = lax.axis_index("grp")
    my_column = lax.axis_index("sp")
    tok, width = grad_out.shape
    top = routes.shape[1]
    hidden = hidden_act.shape[2]
    quarter = hidden // groups
    act_parts = hidden // V
    last = len(CHUNKS) - 1

    codes = route_codes(routes, columns)
    flat = codes.reshape(1, tok * top)
    prob = probs.astype(F32)
    act = hidden_act.reshape(tok * top, hidden)

    def exchange(v):
        return lax.all_to_all(v, "sp", 0, 0, tiled=True)

    held = lax.dynamic_index_in_dim(placement, my_column, 1, keepdims=False) - 2 * my_column
    hops = [[(i, (i + d) % groups) for i in range(groups)] for d in range(groups)]

    near = [(0, 1), (1, 0), (2, 3), (3, 2)]
    far = [(0, 3), (3, 0), (1, 2), (2, 1)]
    g = my_group.astype(jnp.int32)
    order = jnp.stack(
        [jnp.stack([g, 3 - g, g ^ 1, 3 - (g ^ 1)]), jnp.stack([g, g ^ 1, 3 - g, 3 - (g ^ 1)])]
    )

    def first_round(low, high):
        return lax.ppermute(low, "grp", near), lax.ppermute(high, "grp", far)

    def forwarded(keep, came):
        return [(keep[e, quarter:].astype(F32) + came[e][quarter:].astype(F32)).astype(BF16) for e in range(2)]

    def second_round(low, high):
        return lax.ppermute(low, "grp", far), lax.ppermute(high, "grp", near)

    def completed(keep, came, last_came):
        return [
            (keep[e, :quarter].astype(F32) + came[e][:quarter].astype(F32) + last_came[e].astype(F32)).astype(BF16)
            for e in range(2)
        ]

    def wanted(mine):
        out = []
        for d in range(groups):
            which = lax.dynamic_index_in_dim(held, (my_group + d) % groups, 0, keepdims=False)
            out.append(jnp.where(which == 0, mine[0], mine[1]))
        return out

    def hop(sends, d):
        return lax.ppermute(sends[d], "grp", hops[d]) if d else sends[0]

    sources = jnp.stack([(my_group + groups - d) % groups for d in range(groups)]).astype(jnp.int32)

    codes_t = codes.T
    first = send_first(codes_t, flat, prob.reshape(1, tok * top), act, grad_out, columns, CHUNKS[0])
    got = {0: exchange(first)}
    outs = send_rest(codes_t, grad_out, columns, CHUNKS[0], CHUNKS[1:])
    got[0], outs = tie(got[0], outs)
    outs = dict(enumerate(outs, 1))

    starts = [sum(CHUNKS[:c]) for c in range(last + 1)]
    sends, blocks = {}, {}
    state = None
    barrier = lax.optimization_barrier
    for c in range(last + 1):
        if c == 0:
            acts, keep, low, high = weight_first(order, got[0], hidden, CHUNKS[0])
        else:
            got[c], sends[c - 1] = barrier((got[c], sends[c - 1]))
            keep, low, high = weight_rest(acts, got[c], CHUNKS[c])
            pre = lax.ppermute(sends[c - 1][2], "grp", hops[2])
            low, high, pre = barrier((low, high, pre))
            blocks[c - 1] = [sends[c - 1][0], hop(sends[c - 1], 1), pre, hop(sends[c - 1], 3)]
        if c < last:
            got[c + 1] = exchange(outs[c + 1])
            skip = act_parts if c == 0 else 0
            state = project(got[c], down_weight, starts[c], skip, CHUNKS[c], state, False)
        came = first_round(low, high)
        if c == last:
            proj = project(got[last], down_weight, starts[last], 0, CHUNKS[last], state, True)
            back = exchange(proj)
            grad_act, grad_prob = finish(code_column, prob_column, act, back)
        if c >= 1:
            came, blocks[c - 1] = barrier((came, blocks[c - 1]))
        if c == last - 1:
            came, state, code_column, prob_column = barrier(
                (came, state, codes.reshape(tok * top, 1), prob.reshape(tok * top, 1))
            )
        passed = forwarded(keep, came)
        last_came = second_round(*passed)
        if c == last:
            last_came, grad_act, grad_prob = barrier((last_came, grad_act, grad_prob))
        sends[c] = wanted(completed(keep, came, last_came))
    blocks[last] = [hop(sends[last], d) for d in range(groups)]
    own = None
    for c in range(last):
        own = place(sources, blocks[c], own, hidden, width, starts[c] * V)
    for early in ((0, 2, 3), (1,)):
        where = jnp.stack([sources[d] for d in early])
        own = place(where, [blocks[last][d] for d in early], own, hidden, width, starts[last] * V)
    return (
        grad_act.reshape(tok, top, hidden),
        grad_prob.reshape(tok, top),
        own.reshape(1, 1, hidden, width),
    )


def solution(mesh):
    placed = (
        P(("grp", "sp"), None),
        P(("grp", "sp"), None),
        P(("grp", "sp"), None),
        P(("grp", "sp"), None, None),
        P(),
        P("sp", None, None),
    )
    return jax.shard_map(
        shards,
        mesh=mesh,
        in_specs=placed,
        out_specs=(
            P(("grp", "sp"), None, None),
            P(("grp", "sp"), None),
            P("grp", "sp", None, None),
        ),
        check_vma=False,
    )
```
